128 devices in a mesh: row: 8 (over z, core), col: 8 (over x_lo, y), rep: 2 (over x_hi).
Axes of the slice: x: 4 (x_hi: 2, x_lo: 2; x = x_hi * 2 + x_lo), y: 4, z: 4, core: 2. Of those that a mesh axis runs over, the one named last changes fastest.
Arguments:
- pair: bfloat16 [1024, 1024, 128], P('row', 'col'), may hold values from -8 to 8
- w_left: bfloat16 [2, 128, 128], P(None, None, 'rep'), may hold values from -1 to 1
- w_left_gate: bfloat16 [2, 128, 128], P(None, None, 'rep'), may hold values from -0.5 to 0.5
- w_right: bfloat16 [2, 128, 128], P(None, None, 'rep'), may hold values from -0.5 to 0.5
- w_right_gate: bfloat16 [2, 128, 128], P(None, None, 'rep'), may hold values from -0.5 to 0.5
- w_gate: bfloat16 [2, 128, 128], replicated, may hold values from -0.5 to 0.5
- w_out: bfloat16 [2, 128, 128], P(None, 'rep'), may hold values from -0.5 to 0.5
- w_trans_in: bfloat16 [128, 1024], replicated, may hold values from -0.5 to 0.5
- w_trans_out: bfloat16 [512, 128], replicated, may hold values from -0.25 to 0.25
Outputs:
- updated: bfloat16 [1024, 1024, 128], P('row', ('col', 'rep'))
The draws below stay inside these ranges and needn't reach their ends.
All inputs are finite; a program needn't handle non-finite values.
Results may differ from the reference program's by a relative error of at most 0.013.
Values may be sent and summed in bfloat16 or wider, within the bound.
No kernel may reach another device: no remote copies, remote signals or barrier semaphores. Data moves between devices by JAX's collectives and lax.ppermute only.
A program may use at most 192 MiB of HBM per device.

```python
import math
import jax
import jax.numpy as jnp
from jax import lax

C = 128
CH = 128
TR = 512
NPAIR = 1024


def draw_pair(key, part):
    key = jax.random.fold_in(key, 1)
    keys = jax.random.split(key, 4)
    base = jax.random.normal(keys[0], (NPAIR, NPAIR, C), jnp.float32)
    row_scale = jnp.exp(jax.random.uniform(keys[1], (NPAIR, 1, 1), jnp.float32, -1.15, 1.15))
    col_scale = jnp.exp(jax.random.uniform(keys[2], (1, NPAIR, 1), jnp.float32, -0.5, 0.5))
    chan_scale = jnp.exp(jax.random.uniform(keys[3], (1, 1, C), jnp.float32, -1.15, 1.15))
    return jnp.clip(base * row_scale * col_scale * chan_scale, -8.0, 8.0).astype(jnp.bfloat16)


def draw_w_left(key, part):
    key = jax.random.fold_in(key, 2)
    keys = jax.random.split(key, 2)
    base = jax.random.normal(keys[0], (2, C, CH), jnp.float32)
    rising = jnp.exp(math.log(3.0) * (jnp.arange(CH, dtype=jnp.float32) / CH - 0.5))
    spread = jnp.exp(jax.random.uniform(keys[1], (2, 1, CH), jnp.float32, -0.7, 0.7))
    return jnp.clip(base * C ** (-0.5) * rising * spread, -1.0, 1.0).astype(jnp.bfloat16)


def block_levels(own_key, dims, cuts, least, largest):
    level, own = 1.0, jax.random.fold_in(own_key, 6)
    for position, blocks in cuts:
        heights = jnp.exp(jax.random.uniform(jax.random.fold_in(own, position), (blocks,), jnp.float32, least / len(cuts), largest / len(cuts)))
        level = level * jnp.repeat(heights, dims[position] // blocks).reshape([-1 if axis == position else 1 for axis in range(len(dims))])
    return level


def centred(rng, extent, deviation, reach, pieces=(), kind=jnp.bfloat16):
    drawn = jax.random.normal(rng, extent, jnp.float32) * deviation
    if len(pieces) > 0:
        drawn = block_levels(rng, extent, pieces, -0.22, 0.18) * drawn
    return jnp.clip(drawn, min=-reach, max=reach).astype(kind)


def setup_inputs(seed: int = 0) -> dict:
    arg_keys = jax.random.split(jax.random.key(seed), 10)
    pair = draw_pair(jax.random.fold_in(arg_keys[9], 71), 0)
    w_left = draw_w_left(jax.random.fold_in(arg_keys[9], 71), 0)
    w_left_gate = centred(arg_keys[2], (2, C, CH), C ** -0.5, 0.5, ((2, 2),))
    w_right = centred(arg_keys[3], (2, C, CH), C ** -0.5, 0.5, ((2, 2),))
    w_right_gate = centred(arg_keys[4], (2, C, CH), C ** -0.5, 0.5, ((2, 2),))
    w_gate = centred(arg_keys[5], (2, C, C), C ** -0.5, 0.5)
    w_out = centred(arg_keys[6], (2, CH, C), CH ** -0.5, 0.5, ((1, 2),))
    w_trans_in = centred(arg_keys[7], (C, 2 * TR), C ** -0.5, 0.5)
    w_trans_out = centred(arg_keys[8], (TR, C), TR ** -0.5, 0.25)
    return dict(pair=pair, w_left=w_left, w_left_gate=w_left_gate, w_right=w_right, w_right_gate=w_right_gate, w_gate=w_gate, w_out=w_out, w_trans_in=w_trans_in, w_trans_out=w_trans_out)


epsilon = 1e-05

def normalize(values, axis):
    mean_value = lax.optimization_barrier(jnp.mean(values, axis, keepdims=True))
    square_mean = lax.optimization_barrier(jnp.mean(values * values, axis, keepdims=True))
    return (values - mean_value) * lax.rsqrt(square_mean - mean_value * mean_value + epsilon)

def run_blocks(func, total, size):
    starts = jnp.arange(total // size, dtype=jnp.int32) * size
    return lax.map(func, starts)

def update(state, left_w, left_g, right_w, right_g, gate_w, out_w, outgoing):
    npair = state.shape[0]
    size = math.gcd(npair, 64)
    f32 = jnp.float32

    def project(first_row):
        rows = lax.dynamic_slice_in_dim(state, first_row, size, 0)
        normed = normalize(rows, 2).astype(jnp.bfloat16).astype(f32)

        def linear(weight):
            return jnp.einsum('ikd,dc->cik', normed, weight.astype(f32), precision=lax.Precision.HIGHEST)
        left_vals = (jax.nn.sigmoid(linear(left_g)) * linear(left_w)).astype(jnp.bfloat16)
        right_vals = (jax.nn.sigmoid(linear(right_g)) * linear(right_w)).astype(jnp.bfloat16)
        return (left_vals, right_vals)
    lefts, rights = run_blocks(project, npair, size)
    channels = lefts.shape[1]
    left_all = jnp.transpose(lefts, (1, 0, 2, 3)).reshape(channels, npair, npair)
    right_all = jnp.transpose(rights, (1, 0, 2, 3)).reshape(channels, npair, npair)

    def channel_product(operands):
        left_mat = operands[0].astype(f32)
        right_mat = operands[1].astype(f32)
        if outgoing:
            return jnp.dot(left_mat, right_mat.T, precision=lax.Precision.HIGHEST)
        return jnp.dot(left_mat.T, right_mat, precision=lax.Precision.HIGHEST)
    hidden = lax.map(channel_product, (left_all, right_all))

    def finish(first_row):
        rows = lax.dynamic_slice_in_dim(state, first_row, size, 0)
        normed = normalize(rows, 2).astype(jnp.bfloat16).astype(f32)
        gate_values = jax.nn.sigmoid(jnp.einsum('ikd,de->ike', normed, gate_w.astype(f32), precision=lax.Precision.HIGHEST))
        block_hidden = lax.dynamic_slice_in_dim(hidden, first_row, size, 1)
        scaled = normalize(block_hidden, 0).astype(jnp.bfloat16).astype(f32)
        projected = jnp.einsum('cik,cd->ikd', scaled, out_w.astype(f32), precision=lax.Precision.HIGHEST)
        return rows + gate_values * projected
    return run_blocks(finish, npair, size).reshape(state.shape)

def transition(state, w_trans_in, w_trans_out):
    npair = state.shape[0]
    size = math.gcd(npair, 64)
    f32 = jnp.float32
    width = w_trans_out.shape[0]

    def block_fn(first_row):
        rows = lax.dynamic_slice_in_dim(state, first_row, size, 0)
        normed = normalize(rows, 2).astype(jnp.bfloat16).astype(f32)
        inner = jnp.einsum('ijd,de->ije', normed, w_trans_in.astype(f32), precision=lax.Precision.HIGHEST)
        active = (jax.nn.silu(inner[..., :width]) * inner[..., width:]).astype(jnp.bfloat16).astype(f32)
        return (rows + jnp.einsum('ije,ed->ijd', active, w_trans_out.astype(f32), precision=lax.Precision.HIGHEST)).astype(jnp.bfloat16)
    return run_blocks(block_fn, npair, size).reshape(state.shape)

def reference(pair, w_left, w_left_gate, w_right, w_right_gate, w_gate, w_out, w_trans_in, w_trans_out):
    state = pair.astype(jnp.float32)
    state = update(state, w_left[0], w_left_gate[0], w_right[0], w_right_gate[0], w_gate[0], w_out[0], True)
    state = update(state, w_left[1], w_left_gate[1], w_right[1], w_right_gate[1], w_gate[1], w_out[1], False)
    return transition(state, w_trans_in, w_trans_out)
```

```python
import functools

import jax
import jax.numpy as jnp
from jax import lax
from jax.experimental import pallas as pl
from jax.experimental.pallas import tpu as pltpu
from jax.sharding import PartitionSpec as P

epsilon = 1e-05
BF16, F32 = jnp.bfloat16, jnp.float32
NT = (((1,), (1,)), ((), ()))
ROWS = 16
VMEM_BYTES = 48 * 1024 * 1024


def params():
    return pltpu.CompilerParams(vmem_limit_bytes=VMEM_BYTES)


def cost(flops, nbytes, transcendentals=0):
    return pl.CostEstimate(
        flops=int(flops), bytes_accessed=int(nbytes), transcendentals=int(transcendentals)
    )


def normalize(values):
    mean = jnp.mean(values, 0, keepdims=True)
    square = jnp.mean(values * values, 0, keepdims=True)
    return (values - mean) * lax.rsqrt(square - mean * mean + epsilon)


def identity(n):
    rows = lax.broadcasted_iota(jnp.int32, (n, n), 0)
    cols = lax.broadcasted_iota(jnp.int32, (n, n), 1)
    return jnp.where(rows == cols, 1.0, 0.0).astype(BF16)


def gated(half_linear, half_gate):
    return half_linear + half_linear * jnp.tanh(half_gate)


def dot(a, b):
    return jnp.dot(a, b, preferred_element_type=F32)


def front_kernel(pair_ref, w_ref, out_ref, spread):
    eye = identity(128)
    weights = w_ref[...]
    group = 4
    for first in range(0, ROWS, group):
        x = pair_ref[first : first + group].reshape(group * 128, 128)
        state = lax.dot_general(eye, x, NT, preferred_element_type=F32)
        linear = dot(weights, normalize(state).astype(BF16))
        left = gated(linear[0:64], linear[64:128])
        right = gated(linear[128:192], linear[192:256])
        for side, tile in enumerate((left, right)):
            for row in range(group):
                spread[side, pl.ds(first + row, 64, stride=ROWS), :] = tile[
                    :, row * 128 : (row + 1) * 128
                ]
    for side in range(2):
        out_ref[:, side] = spread[side].reshape(64, ROWS, 128).astype(BF16)


def front(pair, weights):
    return pl.pallas_call(
        front_kernel,
        name="front",
        grid=(128 // ROWS,),
        in_specs=[
            pl.BlockSpec((ROWS, 128, 128), lambda s: (s, 0, 0)),
            pl.BlockSpec((256, 128), lambda s: (0, 0)),
        ],
        out_specs=pl.BlockSpec((64, 2, ROWS, 128), lambda s: (0, 0, s, 0)),
        out_shape=jax.ShapeDtypeStruct((64, 2, 128, 128), BF16),
        scratch_shapes=[pltpu.VMEM((2, 64 * ROWS, 128), F32)],
        compiler_params=params(),
        cost_estimate=cost(16384 * 128 * 384 * 2, 12 << 20, 1 << 21),
    )(pair, weights)


def turn_kernel(rep_ref, pair_ref, w_ref, state_ref, gate_ref, spread):
    eye = identity(128)
    weights = w_ref[...]
    spread[...] = pair_ref[...].astype(F32).reshape(128 * ROWS, 128)
    group = 4
    for first in range(0, ROWS, group):
        x = jnp.concatenate(
            [spread[pl.ds(first + r, 128, stride=ROWS), :] for r in range(group)], 0
        ).astype(BF16)
        state = lax.dot_general(eye, x, NT, preferred_element_type=F32)
        half_gate = dot(weights, normalize(state).astype(BF16))
        where = slice(first * 128, (first + group) * 128)
        state_ref[:, where] = state.astype(BF16)
        gate_ref[:, where] = (0.5 + 0.5 * jnp.tanh(half_gate)).astype(BF16)


def turn(rep, pair, weights):
    steps = 64 // ROWS
    return pl.pallas_call(
        turn_kernel,
        name="turn",
        grid_spec=pltpu.PrefetchScalarGridSpec(
            num_scalar_prefetch=1,
            grid=(steps,),
            in_specs=[
                pl.BlockSpec((128, ROWS, 128), lambda s, rep: (0, rep[0] * steps + s, 0)),
                pl.BlockSpec((128, 128), lambda s, rep: (0, 0)),
            ],
            out_specs=[pl.BlockSpec((128, ROWS * 128), lambda s, rep: (0, s))] * 2,
            scratch_shapes=[pltpu.VMEM((128 * ROWS, 128), F32)],
        ),
        out_shape=[jax.ShapeDtypeStruct((128, 8192), BF16)] * 2,
        compiler_params=params(),
        cost_estimate=cost(8192 * 128 * 256 * 2, 6 << 20, 1 << 20),
    )(rep, pair, weights)


def gate_kernel(state_ref, w_ref, gate_ref):
    half_gate = dot(w_ref[...], normalize(state_ref[...]).astype(BF16))
    gate_ref[...] = (0.5 + 0.5 * jnp.tanh(half_gate)).astype(BF16)


def output_gate(state, weights):
    return pl.pallas_call(
        gate_kernel,
        name="output_gate",
        grid=(8,),
        in_specs=[
            pl.BlockSpec((128, 1024), lambda s: (0, s)),
            pl.BlockSpec((128, 128), lambda s: (0, 0)),
        ],
        out_specs=pl.BlockSpec((128, 1024), lambda s: (0, s)),
        out_shape=jax.ShapeDtypeStruct((128, 8192), BF16),
        compiler_params=params(),
        cost_estimate=cost(8192 * 128 * 128 * 2, 6 << 20, 1 << 20),
    )(state, weights)


def product_kernel(left_ref, right_ref, out_ref, *, by_row):
    if by_row:
        left = jnp.concatenate(
            [jnp.concatenate([left_ref[r, q, 0] for q in range(8)], 1) for r in range(2)], 0
        )
        pieces = [
            jnp.concatenate([right_ref[r, q, 0] for q in range(8)], 1) for r in range(8)
        ]
    else:
        left = jnp.concatenate(
            [
                jnp.concatenate([left_ref[p, r, q, 0] for r in range(8)], 1)
                for q in range(2)
                for p in range(2)
            ],
            0,
        )
        pieces = [
            jnp.concatenate(
                [
                    jnp.concatenate([right_ref[p, r, q, 0] for r in range(8)], 1)
                    for p in range(2)
                ],
                0,
            )
            for q in range(8)
        ]
    for q in range(0, 8, 2):
        right = jnp.concatenate(pieces[q : q + 2], 0)
        hidden = lax.dot_general(right, left, NT, preferred_element_type=F32).astype(BF16)
        for qq in range(2):
            for p in range(2):
                rows = slice(qq * 128 + p * 64, qq * 128 + p * 64 + 64)
                for r in range(2):
                    out_ref[p, r, q + qq] = hidden[rows, r * 128 : (r + 1) * 128]


def product(received, by_row):
    if by_row:
        left_spec = pl.BlockSpec((2, 8, 1, 128, 128), lambda s: (s, 0, 0, 0, 0))
        right_spec = pl.BlockSpec((8, 8, 1, 128, 128), lambda s: (0, 0, 1, 0, 0))
        view = received.reshape(8, 8, 2, 128, 128)
    else:
        left_spec = pl.BlockSpec((2, 8, 2, 1, 64, 128), lambda s: (0, 0, s, 0, 0, 0))
        right_spec = pl.BlockSpec((2, 8, 8, 1, 64, 128), lambda s: (0, 0, 0, 1, 0, 0))
        view = received.reshape(2, 8, 8, 2, 64, 128)
    out = pl.pallas_call(
        functools.partial(product_kernel, by_row=by_row),
        name="product_out" if by_row else "product_in",
        grid=(4,),
        in_specs=[left_spec, right_spec],
        out_specs=pl.BlockSpec((2, 2, 8, 64, 128), lambda s: (0, s, 0, 0, 0)),
        out_shape=jax.ShapeDtypeStruct((2, 8, 8, 64, 128), BF16),
        compiler_params=params(),
        cost_estimate=cost(2 << 30, 6 << 20),
    )(view, view)
    return out.reshape(128, 64, 128)


def scale_hidden(hidden_ref, spread):
    values = hidden_ref[...].astype(F32)
    scaled = normalize(values)
    spread[...] = scaled.reshape(128 * ROWS, 128)


def middle_kernel(
    hidden_ref, state_ref, gate_ref, w_out_ref, w_ref, new_ref, out_ref, spread, sides
):
    scale_hidden(hidden_ref, spread)
    w_out = w_out_ref[...]
    weights = w_ref[...]
    group = 4
    for first in range(0, ROWS, group):
        where = slice(first * 128, (first + group) * 128)
        scaled = jnp.concatenate(
            [spread[pl.ds(first + r, 128, stride=ROWS), :] for r in range(group)], 1
        ).astype(BF16)
        projected = dot(w_out, scaled)
        state = state_ref[:, where].astype(F32) + gate_ref[:, where].astype(F32) * projected
        new_ref[:, where] = state
        linear = dot(weights, normalize(state).astype(BF16))
        for half in range(2):
            at = half * 256
            left = gated(linear[at : at + 64], linear[at + 64 : at + 128])
            right = gated(linear[at + 128 : at + 192], linear[at + 192 : at + 256])
            for side, tile in enumerate((left, right)):
                for row in range(group):
                    sides[
                        side, pl.ds(half * 64 * ROWS + first + row, 64, stride=ROWS), :
                    ] = tile[:, row * 128 : (row + 1) * 128]
    for side in range(2):
        out_ref[:, side] = sides[side].reshape(128, ROWS, 128).astype(BF16)


def middle(hidden, state, gate, w_out, weights):
    wide = pl.BlockSpec((128, ROWS * 128), lambda s: (0, s))
    return pl.pallas_call(
        middle_kernel,
        name="middle",
        grid=(64 // ROWS,),
        in_specs=[
            pl.BlockSpec((128, ROWS, 128), lambda s: (0, s, 0)),
            wide,
            wide,
            pl.BlockSpec((128, 128), lambda s: (0, 0)),
            pl.BlockSpec((512, 128), lambda s: (0, 0)),
        ],
        out_specs=[wide, pl.BlockSpec((128, 2, ROWS, 128), lambda s: (0, 0, s, 0))],
        out_shape=[
            jax.ShapeDtypeStruct((128, 8192), F32),
            jax.ShapeDtypeStruct((128, 2, 64, 128), BF16),
        ],
        scratch_shapes=[
            pltpu.VMEM((128 * ROWS, 128), F32),
            pltpu.VMEM((2, 128 * ROWS, 128), F32),
        ],
        compiler_params=params(),
        cost_estimate=cost(8192 * 128 * 640 * 2, 14 << 20, 1 << 21),
    )(hidden, state, gate, w_out, weights)


def finish_kernel(
    hidden_ref, state_ref, gate_ref, w_out_ref, w_in_ref, w_down_ref, out_ref, spread
):
    scale_hidden(hidden_ref, spread)
    w_out = w_out_ref[...]
    group = 4
    for first in range(0, ROWS, group):
        where = slice(first * 128, (first + group) * 128)
        scaled = jnp.concatenate(
            [spread[pl.ds(first + r, 128, stride=ROWS), :] for r in range(group)], 1
        ).astype(BF16)
        projected = dot(w_out, scaled)
        state = state_ref[:, where] + gate_ref[:, where].astype(F32) * projected
        normed = normalize(state).astype(BF16)
        inner = dot(w_in_ref[...], normed)
        active = (gated(inner[:512], inner[:512]) * inner[512:]).astype(BF16)
        updated = state + dot(w_down_ref[...], active)
        for row in range(group):
            spread[pl.ds(first + row, 128, stride=ROWS), :] = updated[
                :, row * 128 : (row + 1) * 128
            ].T
    out_ref[...] = spread[...].reshape(128, ROWS, 128).astype(BF16)


def finish(hidden, state, gate, w_out, w_in, w_down):
    wide = pl.BlockSpec((128, ROWS * 128), lambda s: (0, s))
    return pl.pallas_call(
        finish_kernel,
        name="finish",
        grid=(64 // ROWS,),
        in_specs=[
            pl.BlockSpec((128, ROWS, 128), lambda s: (0, s, 0)),
            wide,
            wide,
            pl.BlockSpec((128, 128), lambda s: (0, 0)),
            pl.BlockSpec((1024, 128), lambda s: (0, 0)),
            pl.BlockSpec((128, 512), lambda s: (0, 0)),
        ],
        out_specs=pl.BlockSpec((128, ROWS, 128), lambda s: (0, s, 0)),
        out_shape=jax.ShapeDtypeStruct((128, 64, 128), BF16),
        scratch_shapes=[pltpu.VMEM((128 * ROWS, 128), F32)],
        compiler_params=params(),
        cost_estimate=cost(8192 * 128 * 1664 * 2, 10 << 20, 1 << 22),
    )(hidden, state, gate, w_out, w_in, w_down)


def exchange(values, axes):
    return lax.all_to_all(values, axes, split_axis=0, concat_axis=0, tiled=True)


def on_device(
    pair, w_left, w_left_gate, w_right, w_right_gate, w_gate, w_out, w_trans_in, w_trans_out
):
    rep = lax.axis_index("rep").astype(jnp.int32).reshape(1)
    everywhere = ("rep", "row", "col")
    projections = (
        jnp.concatenate([w_left, w_left_gate, w_right, w_right_gate], 2) * 0.5
    ).astype(BF16).transpose(0, 2, 1)
    gates = (w_gate * 0.5).astype(BF16).transpose(0, 2, 1)
    shared = lax.all_gather(
        jnp.concatenate([projections[1], w_out.reshape(128, 128)], 0), "rep", axis=0
    )
    w_second = shared[:, :256].reshape(512, 128)
    w_outs = shared[:, 256:].reshape(2, 2, 64, 128).transpose(1, 3, 0, 2).reshape(2, 128, 128)
    scale = jnp.where(jnp.arange(1024) < 512, 0.5, 1.0).astype(BF16)
    w_in = (w_trans_in * scale).T
    w_down = w_trans_out.T

    sides = front(pair, projections[0])
    received = exchange(sides, ("row", "col"))
    state, gate = turn(rep, pair, gates[0])
    hidden = exchange(product(received, True), everywhere)
    state, sides = middle(hidden, state, gate, w_outs[0], w_second)
    received = exchange(sides, everywhere)
    gate = output_gate(state, gates[1])
    hidden = exchange(product(received, False), everywhere)
    return finish(hidden, state, gate, w_outs[1], w_in, w_down)


def solution(mesh):
    placed = (
        P("row", "col", None),
        P(None, None, "rep"),
        P(None, None, "rep"),
        P(None, None, "rep"),
        P(None, None, "rep"),
        P(),
        P(None, "rep", None),
        P(),
        P(),
    )
    return jax.shard_map(
        on_device,
        mesh=mesh,
        in_specs=placed,
        out_specs=P("row", ("col", "rep"), None),
        check_vma=False,
    )
```

```python
import functools

import jax
import jax.numpy as jnp
from jax import lax
from jax.experimental import pallas as pl
from jax.experimental.pallas import tpu as pltpu
from jax.sharding import PartitionSpec as P

epsilon = 1e-05
BF16, F32 = jnp.bfloat16, jnp.float32
NT = (((1,), (1,)), ((), ()))
TN = (((0,), (0,)), ((), ()))
ROWS = 16
PITCH = 17
FRONT_ROWS, FRONT_PITCH = 32, 33
VMEM_BYTES = 60 * 1024 * 1024
FINISH_BYTES = 36 * 1024 * 1024


def params(nbytes=VMEM_BYTES):
    return pltpu.CompilerParams(vmem_limit_bytes=nbytes)


def cost(flops, nbytes, transcendentals=0):
    return pl.CostEstimate(
        flops=int(flops), bytes_accessed=int(nbytes), transcendentals=int(transcendentals)
    )


def normalize(values):
    mean = jnp.mean(values, 0, keepdims=True)
    square = jnp.mean(values * values, 0, keepdims=True)
    return (values - mean) * lax.rsqrt(square - mean * mean + epsilon)


def gated(half_linear, half_gate):
    return half_linear + half_linear * jnp.tanh(half_gate)


def dot(a, b):
    return jnp.dot(a, b, preferred_element_type=F32)


def front_kernel(pair_ref, wl_ref, wlg_ref, wr_ref, wrg_ref, out_ref, spread):
    weights = jnp.concatenate([wl_ref[0], wlg_ref[0], wr_ref[0], wrg_ref[0]], 0) * 0.5
    weights = weights.astype(BF16)
    group = 4
    for first in range(0, FRONT_ROWS, group):
        state = jnp.concatenate(
            [pair_ref[first + row].T for row in range(group)], 1
        ).astype(F32)
        linear = dot(weights, normalize(state).astype(BF16))
        left = gated(linear[0:64], linear[64:128])
        right = gated(linear[128:192], linear[192:256])
        for side, tile in enumerate((left, right)):
            for row in range(group):
                spread[side, pl.ds(first + row, 64, stride=FRONT_PITCH), :] = tile[
                    :, row * 128 : (row + 1) * 128
                ]
    for side in range(2):
        for c in range(64):
            at = c * FRONT_PITCH
            out_ref[c, side] = spread[side, at : at + FRONT_ROWS, :].astype(BF16)


def front(pair, weights):
    return pl.pallas_call(
        front_kernel,
        name="front",
        grid=(128 // FRONT_ROWS,),
        in_specs=[pl.BlockSpec((FRONT_ROWS, 128, 128), lambda s: (s, 0, 0))]
        + [pl.BlockSpec((1, 64, 128), lambda s: (0, 0, 0))] * 4,
        out_specs=pl.BlockSpec((64, 2, FRONT_ROWS, 128), lambda s: (0, 0, s, 0)),
        out_shape=jax.ShapeDtypeStruct((64, 2, 128, 128), BF16),
        scratch_shapes=[pltpu.VMEM((2, 64 * FRONT_PITCH, 128), F32)],
        compiler_params=params(),
        cost_estimate=cost(16384 * 128 * 384 * 2, 12 << 20, 1 << 21),
    )(pair, *weights)


def turn_kernel(rep_ref, pair_ref, w_ref, state_ref, gate_ref, spread):
    weights = w_ref[...]
    for i in range(128):
        spread[i * FRONT_PITCH : i * FRONT_PITCH + FRONT_ROWS, :] = pair_ref[i].astype(F32)
    group = 4
    for first in range(0, FRONT_ROWS, group):
        state = jnp.concatenate(
            [spread[pl.ds(first + r, 128, stride=FRONT_PITCH), :].T for r in range(group)], 1
        )
        half_gate = dot(weights, normalize(state).astype(BF16))
        where = slice(first * 128, (first + group) * 128)
        state_ref[:, where] = state.astype(BF16)
        gate_ref[:, where] = (0.5 + 0.5 * jnp.tanh(half_gate)).astype(BF16)


def turn(rep, pair, weights):
    steps = 64 // FRONT_ROWS
    return pl.pallas_call(
        turn_kernel,
        name="turn",
        grid_spec=pltpu.PrefetchScalarGridSpec(
            num_scalar_prefetch=1,
            grid=(steps,),
            in_specs=[
                pl.BlockSpec((128, FRONT_ROWS, 128), lambda s, rep: (0, rep[0] * steps + s, 0)),
                pl.BlockSpec((128, 128), lambda s, rep: (0, 0)),
            ],
            out_specs=[pl.BlockSpec((128, FRONT_ROWS * 128), lambda s, rep: (0, s))] * 2,
            scratch_shapes=[pltpu.VMEM((128 * FRONT_PITCH, 128), F32)],
        ),
        out_shape=[jax.ShapeDtypeStruct((128, 8192), BF16)] * 2,
        compiler_params=params(),
        cost_estimate=cost(8192 * 128 * 256 * 2, 6 << 20, 1 << 20),
    )(rep, pair, weights)


def gate_kernel(state_ref, w_ref, gate_ref):
    half_gate = dot(w_ref[...], normalize(state_ref[...]).astype(BF16))
    gate_ref[...] = (0.5 + 0.5 * jnp.tanh(half_gate)).astype(BF16)


def output_gate(state, weights):
    return pl.pallas_call(
        gate_kernel,
        name="output_gate",
        grid=(8,),
        in_specs=[
            pl.BlockSpec((128, 1024), lambda s: (0, s)),
            pl.BlockSpec((128, 128), lambda s: (0, 0)),
        ],
        out_specs=pl.BlockSpec((128, 1024), lambda s: (0, s)),
        out_shape=jax.ShapeDtypeStruct((128, 8192), BF16),
        compiler_params=params(),
        cost_estimate=cost(8192 * 128 * 128 * 2, 6 << 20, 1 << 20),
    )(state, weights)


def product_kernel(left_ref, *refs, by_row):
    *right_refs, out_ref = refs
    if by_row:
        left = [jnp.concatenate([left_ref[r, q, 0] for q in range(8)], 1) for r in range(4)]
        pieces = [
            jnp.concatenate([right_refs[r // 2][r % 2, q, 0] for q in range(8)], 1)
            for r in range(8)
        ]
    else:
        left = [
            jnp.concatenate([left_ref[p, r, q, 0] for r in range(8)], 1)
            for q in range(4)
            for p in range(2)
        ]
        pieces = [
            jnp.concatenate(
                [
                    jnp.concatenate([right_refs[q // 2][p, r, q % 2, 0] for r in range(8)], 1)
                    for p in range(2)
                ],
                0,
            )
            for q in range(8)
        ]
    left = jnp.concatenate(left, 0)
    for q in range(0, 8, 2):
        right = jnp.concatenate(pieces[q : q + 2], 0)
        hidden = lax.dot_general(right, left, NT, preferred_element_type=F32).astype(BF16)
        for qq in range(2):
            for p in range(2):
                rows = slice(qq * 128 + p * 64, qq * 128 + p * 64 + 64)
                for r in range(4):
                    out_ref[p, r, q + qq] = hidden[rows, r * 128 : (r + 1) * 128]


def product(received, by_row):
    if by_row:
        left_spec = pl.BlockSpec((4, 8, 1, 128, 128), lambda s: (s, 0, 0, 0, 0))
        right_specs = [
            pl.BlockSpec((2, 8, 1, 128, 128), lambda s, i=i: (i, 0, 1, 0, 0)) for i in range(4)
        ]
        view = received.reshape(8, 8, 2, 128, 128)
    else:
        left_spec = pl.BlockSpec((2, 8, 4, 1, 64, 128), lambda s: (0, 0, s, 0, 0, 0))
        right_specs = [
            pl.BlockSpec((2, 8, 2, 1, 64, 128), lambda s, i=i: (0, 0, i, 1, 0, 0))
            for i in range(4)
        ]
        view = received.reshape(2, 8, 8, 2, 64, 128)
    out = pl.pallas_call(
        functools.partial(product_kernel, by_row=by_row),
        name="product_out" if by_row else "product_in",
        grid=(2,),
        in_specs=[left_spec] + right_specs,
        out_specs=pl.BlockSpec((2, 4, 8, 64, 128), lambda s: (0, s, 0, 0, 0)),
        out_shape=jax.ShapeDtypeStruct((2, 8, 8, 64, 128), BF16),
        compiler_params=params(),
        cost_estimate=cost(2 << 30, 6 << 20),
    )(*[view] * 5)
    return out.reshape(128, 64, 128)


def scale_hidden(hidden_ref, spread):
    total = jnp.zeros((ROWS, 128), F32)
    squares = jnp.zeros((ROWS, 128), F32)
    for c in range(128):
        values = hidden_ref[c].astype(F32)
        total += values
        squares += values * values
    mean = total * (1.0 / 128)
    factor = lax.rsqrt(squares * (1.0 / 128) - mean * mean + epsilon)
    for c in range(128):
        spread[c * PITCH : c * PITCH + ROWS, :] = (
            hidden_ref[c].astype(F32) - mean
        ) * factor
    return jnp.concatenate(
        [spread[pl.ds(r, 128, stride=PITCH), :] for r in range(ROWS)], 1
    ).astype(BF16)


def both_halves(rep_ref, mine, other):
    first = rep_ref[0] == 0
    return jnp.concatenate(
        [jnp.where(first, mine, other), jnp.where(first, other, mine)], 0
    )


def middle_kernel(
    rep_ref, hidden_ref, state_ref, gate_ref, mine_ref, other_ref, new_ref, out_ref,
    spread, sides,
):
    w_out = both_halves(rep_ref, mine_ref[256:320], other_ref[256:320])
    weights = both_halves(rep_ref, mine_ref[:256], other_ref[:256])
    scaled = scale_hidden(hidden_ref, spread)
    projected = lax.dot_general(w_out, scaled, TN, preferred_element_type=F32)
    state = state_ref[...].astype(F32) + gate_ref[...].astype(F32) * projected
    new_ref[...] = state
    linear = dot(weights, normalize(state).astype(BF16))
    for half in range(2):
        at = half * 256
        left = gated(linear[at : at + 64], linear[at + 64 : at + 128])
        right = gated(linear[at + 128 : at + 192], linear[at + 192 : at + 256])
        for side, tile in enumerate((left, right)):
            for row in range(ROWS):
                sides[side, pl.ds(half * 64 * PITCH + row, 64, stride=PITCH), :] = tile[
                    :, row * 128 : (row + 1) * 128
                ]
    for side in range(2):
        for c in range(128):
            out_ref[c, side] = sides[side, c * PITCH : c * PITCH + ROWS, :].astype(BF16)


def middle(rep, hidden, state, gate, mine, other):
    wide = pl.BlockSpec((128, ROWS * 128), lambda s, rep: (0, s))
    halves = pl.BlockSpec((384, 128), lambda s, rep: (0, 0))
    return pl.pallas_call(
        middle_kernel,
        name="middle",
        grid_spec=pltpu.PrefetchScalarGridSpec(
            num_scalar_prefetch=1,
            grid=(64 // ROWS,),
            in_specs=[
                pl.BlockSpec((128, ROWS, 128), lambda s, rep: (0, s, 0)),
                wide,
                wide,
                halves,
                halves,
            ],
            out_specs=[wide, pl.BlockSpec((128, 2, ROWS, 128), lambda s, rep: (0, 0, s, 0))],
            scratch_shapes=[
                pltpu.VMEM((128 * PITCH, 128), F32),
                pltpu.VMEM((2, 128 * PITCH, 128), F32),
            ],
        ),
        out_shape=[
            jax.ShapeDtypeStruct((128, 8192), F32),
            jax.ShapeDtypeStruct((128, 2, 64, 128), BF16),
        ],
        compiler_params=params(),
        cost_estimate=cost(8192 * 128 * 640 * 2, 14 << 20, 1 << 21),
    )(rep, hidden, state, gate, mine, other)


def finish_kernel(
    rep_ref, hidden_ref, state_ref, gate_ref, mine_ref, other_ref, w_in_ref, w_down_ref,
    out_ref, spread, state_scr, normed_scr,
):
    w_out = both_halves(rep_ref, mine_ref[320:], other_ref[320:])
    scaled = scale_hidden(hidden_ref, spread)
    projected = lax.dot_general(w_out, scaled, TN, preferred_element_type=F32)
    state = state_ref[...] + gate_ref[...].astype(F32) * projected
    state_scr[...] = state
    normed_scr[...] = normalize(state).astype(BF16)
    group = 8
    for first in range(0, ROWS, group):
        where = slice(first * 128, (first + group) * 128)
        normed = normed_scr[:, where]
        half_gate = dot(w_in_ref[:512], normed)
        linear = dot(w_in_ref[512:], normed)
        active = (gated(half_gate, half_gate) * linear).astype(BF16)
        updated = state_scr[:, where] + dot(w_down_ref[...], active)
        for row in range(group):
            spread[pl.ds(first + row, 128, stride=PITCH), :] = updated[
                :, row * 128 : (row + 1) * 128
            ].T
    for i in range(128):
        out_ref[i] = spread[i * PITCH : i * PITCH + ROWS, :].astype(BF16)


def finish(rep, hidden, state, gate, mine, other, w_in, w_down):
    wide = pl.BlockSpec((128, ROWS * 128), lambda s, rep: (0, s))
    halves = pl.BlockSpec((384, 128), lambda s, rep: (0, 0))
    return pl.pallas_call(
        finish_kernel,
        name="finish",
        grid_spec=pltpu.PrefetchScalarGridSpec(
            num_scalar_prefetch=1,
            grid=(64 // ROWS,),
            in_specs=[
                pl.BlockSpec((128, ROWS, 128), lambda s, rep: (0, s, 0)),
                wide,
                wide,
                halves,
                halves,
                pl.BlockSpec((1024, 128), lambda s, rep: (0, 0)),
                pl.BlockSpec((128, 512), lambda s, rep: (0, 0)),
            ],
            out_specs=pl.BlockSpec((128, ROWS, 128), lambda s, rep: (0, s, 0)),
            scratch_shapes=[
                pltpu.VMEM((128 * PITCH, 128), F32),
                pltpu.VMEM((128, ROWS * 128), F32),
                pltpu.VMEM((128, ROWS * 128), BF16),
            ],
        ),
        out_shape=jax.ShapeDtypeStruct((128, 64, 128), BF16),
        compiler_params=params(FINISH_BYTES),
        cost_estimate=cost(8192 * 128 * 1664 * 2, 10 << 20, 1 << 22),
    )(rep, hidden, state, gate, mine, other, w_in, w_down)


def exchange(values, axes):
    return lax.all_to_all(values, axes, split_axis=0, concat_axis=0, tiled=True)


def on_device(
    pair, w_left, w_left_gate, w_right, w_right_gate, w_gate, w_out, w_trans_in, w_trans_out
):
    rep = lax.axis_index("rep").astype(jnp.int32).reshape(1)
    everywhere = ("rep", "row", "col")
    projections = [
        w.transpose(0, 2, 1) for w in (w_left, w_left_gate, w_right, w_right_gate)
    ]
    sides = front(pair, projections)
    received = exchange(sides, ("row", "col"))

    mine = jnp.concatenate(
        [(w[1] * 0.5).astype(BF16) for w in projections] + [w_out[0], w_out[1]], 0
    )
    other = lax.ppermute(mine, "rep", [(0, 1), (1, 0)])
    gates = (w_gate * 0.5).astype(BF16).transpose(0, 2, 1)
    scale = jnp.where(jnp.arange(1024) < 512, 0.5, 1.0).astype(BF16)
    w_in = (w_trans_in * scale).T
    w_down = w_trans_out.T
    state, gate = turn(rep, pair, gates[0])
    received, state, gate, gates, w_in, w_down, mine, other = lax.optimization_barrier(
        (received, state, gate, gates, w_in, w_down, mine, other)
    )

    hidden = exchange(product(received, True), everywhere)
    state, sides = middle(rep, hidden, state, gate, mine, other)
    received = exchange(sides, everywhere)
    gate = output_gate(state, gates[1])
    received, gate = lax.optimization_barrier((received, gate))
    hidden = exchange(product(received, False), everywhere)
    return finish(rep, hidden, state, gate, mine, other, w_in, w_down)


def solution(mesh):
    placed = (
        P("row", "col", None),
        P(None, None, "rep"),
        P(None, None, "rep"),
        P(None, None, "rep"),
        P(None, None, "rep"),
        P(),
        P(None, "rep", None),
        P(),
        P(),
    )
    return jax.shard_map(
        on_device,
        mesh=mesh,
        in_specs=placed,
        out_specs=P("row", ("col", "rep"), None),
        check_vma=False,
    )
```

```python
import functools

import jax
import jax.numpy as jnp
from jax import lax
from jax.experimental import pallas as pl
from jax.experimental.pallas import tpu as pltpu
from jax.sharding import PartitionSpec as P

epsilon = 1e-05
BF16, F32 = jnp.bfloat16, jnp.float32
VMEM = pl.BlockSpec(memory_space=pltpu.VMEM)
SMEM = pl.BlockSpec(memory_space=pltpu.SMEM)
ANY = pl.BlockSpec(memory_space=pl.ANY)
NT = (((1,), (1,)), ((), ()))
TN = (((0,), (0,)), ((), ()))
ROWS = 16
PITCH = 17
FRONT_ROWS, FRONT_PITCH = 32, 33


PRODUCT_MIB, MIDDLE_MIB, FINISH_MIB = 24, 36, 36


def params(mebibytes):
    return pltpu.CompilerParams(vmem_limit_bytes=mebibytes * 1024 * 1024)


def cost(flops, nbytes, transcendentals=0):
    return pl.CostEstimate(
        flops=int(flops), bytes_accessed=int(nbytes), transcendentals=int(transcendentals)
    )


def normalize(values):
    mean = jnp.mean(values, 0, keepdims=True)
    square = jnp.mean(values * values, 0, keepdims=True)
    return (values - mean) * lax.rsqrt(square - mean * mean + epsilon)


def gated(half_linear, half_gate):
    return half_linear + half_linear * jnp.tanh(half_gate)


def dot(a, b):
    return jnp.dot(a, b, preferred_element_type=F32)


def front_kernel(pair_ref, wl_ref, wlg_ref, wr_ref, wrg_ref, out_ref, spread):
    weights = jnp.concatenate([wl_ref[0], wlg_ref[0], wr_ref[0], wrg_ref[0]], 0) * 0.5
    weights = weights.astype(BF16)
    group = 4
    for first in range(0, FRONT_ROWS, group):
        state = jnp.concatenate(
            [pair_ref[first + row].T for row in range(group)], 1
        ).astype(F32)
        linear = dot(weights, normalize(state).astype(BF16))
        left = gated(linear[0:64], linear[64:128])
        right = gated(linear[128:192], linear[192:256])
        for side, tile in enumerate((left, right)):
            for row in range(group):
                spread[side, pl.ds(first + row, 64, stride=FRONT_PITCH), :] = tile[
                    :, row * 128 : (row + 1) * 128
                ]
    for side in range(2):
        for c in range(64):
            at = c * FRONT_PITCH
            out_ref[c, side] = spread[side, at : at + FRONT_ROWS, :].astype(BF16)


def front(pair, weights):
    return pl.pallas_call(
        front_kernel,
        name="front",
        grid=(128 // FRONT_ROWS,),
        in_specs=[pl.BlockSpec((FRONT_ROWS, 128, 128), lambda s: (s, 0, 0))]
        + [pl.BlockSpec((1, 64, 128), lambda s: (0, 0, 0))] * 4,
        out_specs=pl.BlockSpec((64, 2, FRONT_ROWS, 128), lambda s: (0, 0, s, 0)),
        out_shape=pltpu.HBM((64, 2, 128, 128), BF16),
        scratch_shapes=[pltpu.VMEM((2, 64 * FRONT_PITCH, 128), F32)],
        compiler_params=params(60),
        cost_estimate=cost(16384 * 128 * 384 * 2, 12 << 20, 1 << 21),
    )(pair, *weights)


def turn_kernel(rep_ref, pair_ref, w_ref, state_ref, gate_ref, spread):
    weights = w_ref[...]
    for i in range(128):
        spread[i * FRONT_PITCH : i * FRONT_PITCH + FRONT_ROWS, :] = pair_ref[i].astype(F32)
    group = 4
    for first in range(0, FRONT_ROWS, group):
        state = jnp.concatenate(
            [spread[pl.ds(first + r, 128, stride=FRONT_PITCH), :].T for r in range(group)], 1
        )
        half_gate = dot(weights, normalize(state).astype(BF16))
        where = slice(first * 128, (first + group) * 128)
        state_ref[:, where] = state.astype(BF16)
        gate_ref[:, where] = (0.5 + 0.5 * jnp.tanh(half_gate)).astype(BF16)


def turn(rep, pair, weights):
    steps = 64 // FRONT_ROWS
    return pl.pallas_call(
        turn_kernel,
        name="turn",
        grid_spec=pltpu.PrefetchScalarGridSpec(
            num_scalar_prefetch=1,
            grid=(steps,),
            in_specs=[
                pl.BlockSpec((128, FRONT_ROWS, 128), lambda s, rep: (0, rep[0] * steps + s, 0)),
                pl.BlockSpec((128, 128), lambda s, rep: (0, 0)),
            ],
            out_specs=[pl.BlockSpec((128, FRONT_ROWS * 128), lambda s, rep: (0, s))] * 2,
            scratch_shapes=[pltpu.VMEM((128 * FRONT_PITCH, 128), F32)],
        ),
        out_shape=[pltpu.HBM((128, 8192), BF16)] * 2,
        compiler_params=params(36),
        cost_estimate=cost(8192 * 128 * 256 * 2, 6 << 20, 1 << 20),
    )(rep, pair, weights)


def product_kernel(got_ref, out_ref, products, sems, *, by_row):
    def block(n, side):
        if by_row:
            return jnp.concatenate([got_ref[n, q, side] for q in range(8)], 1)
        return jnp.concatenate(
            [
                jnp.concatenate([got_ref[p, r, n, side] for r in range(8)], 1)
                for p in range(2)
            ],
            0,
        )

    copies = []
    for step in range(4):
        left = jnp.concatenate([block(2 * step, 0), block(2 * step + 1, 0)], 0)
        for q in range(0, 8, 2):
            right = jnp.concatenate([block(q, 1), block(q + 1, 1)], 0)
            hidden = lax.dot_general(right, left, NT, preferred_element_type=F32).astype(BF16)
            for qq in range(2):
                for p in range(2):
                    at = qq * 128 + p * 64
                    for r in range(2):
                        products[p, 2 * step + r, q + qq] = hidden[
                            at : at + 64, r * 128 : (r + 1) * 128
                        ]
        for p in range(2):
            rows = pl.ds(2 * step, 2)
            copy = pltpu.make_async_copy(
                products.at[p, rows], out_ref.at[p, rows], sems.at[step, p]
            )
            copy.start()
            copies.append(copy)
    for copy in copies:
        copy.wait()


def product(received, by_row):
    out = pl.pallas_call(
        functools.partial(product_kernel, by_row=by_row),
        name="product_out" if by_row else "product_in",
        in_specs=[VMEM],
        out_specs=ANY,
        out_shape=pltpu.HBM((2, 8, 8, 64, 128), BF16),
        scratch_shapes=[
            pltpu.VMEM((2, 8, 8, 64, 128), BF16),
            pltpu.SemaphoreType.DMA((4, 2)),
        ],
        compiler_params=params(PRODUCT_MIB),
        cost_estimate=cost(2 << 30, 6 << 20),
    )(received)
    return out.reshape(128, 64, 128)


def scale_hidden(hidden_ref, first, spread):
    total = jnp.zeros((ROWS, 128), F32)
    squares = jnp.zeros((ROWS, 128), F32)
    for c in range(128):
        values = hidden_ref[c, first : first + ROWS].astype(F32)
        total += values
        squares += values * values
    mean = total * (1.0 / 128)
    factor = lax.rsqrt(squares * (1.0 / 128) - mean * mean + epsilon)
    for c in range(128):
        spread[c * PITCH : c * PITCH + ROWS, :] = (
            hidden_ref[c, first : first + ROWS].astype(F32) - mean
        ) * factor
    return jnp.concatenate(
        [spread[pl.ds(r, 128, stride=PITCH), :] for r in range(ROWS)], 1
    ).astype(BF16)


def both_halves(rep_ref, mine, other):
    first = rep_ref[0] == 0
    return jnp.concatenate(
        [jnp.where(first, mine, other), jnp.where(first, other, mine)], 0
    )


def middle_kernel(
    rep_ref, hidden_ref, state_ref, gate_ref, mine_ref, other_ref, w_gate_ref, new_ref,
    new_gate_ref, out_ref, spread, sides, packed, old_state, old_gate, sems, load_sems,
):
    loads = []
    for first in range(0, 64, ROWS):
        part = pl.ds(first * 128, ROWS * 128)
        loads.append(
            [
                pltpu.make_async_copy(
                    source.at[:, part], target.at[:, part], load_sems.at[n, first // ROWS]
                )
                for n, (source, target) in enumerate(
                    ((state_ref, old_state), (gate_ref, old_gate))
                )
            ]
        )
    for pair_of_loads in loads:
        for load in pair_of_loads:
            load.start()
    w_out = both_halves(rep_ref, mine_ref[256:320], other_ref[256:320])
    weights = both_halves(rep_ref, mine_ref[:256], other_ref[:256])
    copies = []
    for first in range(0, 64, ROWS):
        where = slice(first * 128, (first + ROWS) * 128)
        scaled = scale_hidden(hidden_ref, first, spread)
        projected = lax.dot_general(w_out, scaled, TN, preferred_element_type=F32)
        for load in loads[first // ROWS]:
            load.wait()
        state = old_state[:, where].astype(F32) + old_gate[:, where].astype(F32) * projected
        new_ref[:, where] = state.astype(new_ref.dtype)
        normed = normalize(state).astype(BF16)
        half_gate = dot(w_gate_ref[...], normed)
        new_gate_ref[:, where] = (0.5 + 0.5 * jnp.tanh(half_gate)).astype(BF16)
        linear = dot(weights, normed)
        for half in range(2):
            at = half * 256
            left = gated(linear[at : at + 64], linear[at + 64 : at + 128])
            right = gated(linear[at + 128 : at + 192], linear[at + 192 : at + 256])
            for side, tile in enumerate((left, right)):
                for row in range(ROWS):
                    sides[side, pl.ds(half * 64 * PITCH + row, 64, stride=PITCH), :] = tile[
                        :, row * 128 : (row + 1) * 128
                    ]
        for side in range(2):
            for c in range(128):
                packed[c, side, first : first + ROWS] = sides[
                    side, c * PITCH : c * PITCH + ROWS, :
                ].astype(BF16)
        rows = pl.ds(first, ROWS)
        copy = pltpu.make_async_copy(
            packed.at[:, :, rows], out_ref.at[:, :, rows], sems.at[first // ROWS]
        )
        copy.start()
        copies.append(copy)
    for copy in copies:
        copy.wait()


def middle(rep, hidden, state, gate, mine, other, w_gate):
    return pl.pallas_call(
        middle_kernel,
        name="middle",
        in_specs=[SMEM, VMEM, ANY, ANY, VMEM, VMEM, VMEM],
        out_specs=[VMEM, VMEM, ANY],
        out_shape=[
            jax.ShapeDtypeStruct((128, 8192), BF16),
            jax.ShapeDtypeStruct((128, 8192), BF16),
            pltpu.HBM((128, 2, 64, 128), BF16),
        ],
        scratch_shapes=[
            pltpu.VMEM((128 * PITCH, 128), F32),
            pltpu.VMEM((2, 128 * PITCH, 128), F32),
            pltpu.VMEM((128, 2, 64, 128), BF16),
            pltpu.VMEM((128, 8192), BF16),
            pltpu.VMEM((128, 8192), BF16),
            pltpu.SemaphoreType.DMA((64 // ROWS,)),
            pltpu.SemaphoreType.DMA((2, 64 // ROWS)),
        ],
        compiler_params=params(MIDDLE_MIB),
        cost_estimate=cost(8192 * 128 * 640 * 2, 14 << 20, 1 << 21),
    )(rep, hidden, state, gate, mine, other, w_gate)


def finish_kernel(
    rep_ref, hidden_ref, state_ref, gate_ref, mine_ref, other_ref, w_in_ref, w_down_ref,
    out_ref, spread, state_scr, normed_scr, turned, packed, sems,
):
    w_out = both_halves(rep_ref, mine_ref[320:], other_ref[320:])
    w_half_gate = (w_in_ref[:512] * 0.5).astype(BF16)
    group = 8
    copies = []
    for first in range(0, 64, ROWS):
        where = slice(first * 128, (first + ROWS) * 128)
        scaled = scale_hidden(hidden_ref, first, spread)
        projected = lax.dot_general(w_out, scaled, TN, preferred_element_type=F32)
        state = state_ref[:, where].astype(F32) + gate_ref[:, where].astype(F32) * projected
        state_scr[...] = state
        normed_scr[...] = normalize(state).astype(BF16)
        for start in range(0, ROWS, group):
            part = slice(start * 128, (start + group) * 128)
            normed = normed_scr[:, part]
            half_gate = dot(w_half_gate, normed)
            linear = dot(w_in_ref[512:], normed)
            active = (gated(half_gate, half_gate) * linear).astype(BF16)
            updated = state_scr[:, part] + dot(w_down_ref[...], active)
            for row in range(group):
                turned[pl.ds(start + row, 128, stride=PITCH), :] = updated[
                    :, row * 128 : (row + 1) * 128
                ].T
        for i in range(128):
            packed[i, first : first + ROWS] = turned[i * PITCH : i * PITCH + ROWS, :].astype(
                BF16
            )
        rows = pl.ds(first, ROWS)
        copy = pltpu.make_async_copy(
            packed.at[:, rows], out_ref.at[:, rows], sems.at[first // ROWS]
        )
        copy.start()
        copies.append(copy)
    for copy in copies:
        copy.wait()


def finish(rep, hidden, state, gate, mine, other, w_in, w_down):
    return pl.pallas_call(
        finish_kernel,
        name="finish",
        in_specs=[SMEM] + [VMEM] * 7,
        out_specs=ANY,
        out_shape=pltpu.HBM((128, 64, 128), BF16),
        scratch_shapes=[
            pltpu.VMEM((128 * PITCH, 128), F32),
            pltpu.VMEM((128, ROWS * 128), F32),
            pltpu.VMEM((128, ROWS * 128), BF16),
            pltpu.VMEM((128 * PITCH, 128), F32),
            pltpu.VMEM((128, 64, 128), BF16),
            pltpu.SemaphoreType.DMA((64 // ROWS,)),
        ],
        compiler_params=params(FINISH_MIB),
        cost_estimate=cost(8192 * 128 * 1664 * 2, 10 << 20, 1 << 22),
    )(rep, hidden, state, gate, mine, other, w_in, w_down)


def exchange(values, axes):
    return lax.all_to_all(values, axes, split_axis=0, concat_axis=0, tiled=True)


def near(values):
    return pltpu.with_memory_space_constraint(values, pltpu.VMEM)


def far(values):
    return pltpu.with_memory_space_constraint(values, pltpu.HBM)


def on_device(
    pair, w_left, w_left_gate, w_right, w_right_gate, w_gate, w_out, w_trans_in, w_trans_out
):
    rep = lax.axis_index("rep").astype(jnp.int32).reshape(1)
    everywhere = ("rep", "row", "col")
    projections = [
        w.transpose(0, 2, 1) for w in (w_left, w_left_gate, w_right, w_right_gate)
    ]
    sides = front(pair, projections)
    sides, rep = lax.optimization_barrier((sides, rep))
    received = exchange(sides, ("row", "col"))

    products = product(near(received.reshape(8, 8, 2, 128, 128)), True)
    products, pair, w_gate, w_out, w_trans_in, w_trans_out, *projections = (
        lax.optimization_barrier(
            (products, pair, w_gate, w_out, w_trans_in, w_trans_out, *projections)
        )
    )
    hidden = exchange(products, everywhere)

    mine = jnp.concatenate(
        [(w[1] * 0.5).astype(BF16) for w in projections] + [w_out[0], w_out[1]], 0
    )
    other = lax.ppermute(mine, "rep", [(0, 1), (1, 0)])
    gates = (w_gate * 0.5).astype(BF16).transpose(0, 2, 1)
    w_in = w_trans_in.T
    w_down = w_trans_out.T
    state, gate = turn(rep, pair, gates[0])
    hidden, state, gate, gates, w_in, w_down, mine, other = lax.optimization_barrier(
        (hidden, state, gate, gates, w_in, w_down, mine, other)
    )

    state, gate, sides = middle(rep, near(hidden), far(state), far(gate), mine, other, gates[1])
    received = exchange(sides, everywhere)
    hidden = exchange(product(near(received.reshape(2, 8, 8, 2, 64, 128)), False), everywhere)
    return finish(rep, near(hidden), state, gate, mine, other, w_in, w_down)


def solution(mesh):
    placed = (
        P("row", "col", None),
        P(None, None, "rep"),
        P(None, None, "rep"),
        P(None, None, "rep"),
        P(None, None, "rep"),
        P(),
        P(None, "rep", None),
        P(),
        P(),
    )
    return jax.shard_map(
        on_device,
        mesh=mesh,
        in_specs=placed,
        out_specs=P("row", ("col", "rep"), None),
        check_vma=False,
    )
```

```python
import functools

import jax
import jax.numpy as jnp
from jax import lax
from jax.experimental import pallas as pl
from jax.experimental.pallas import tpu as pltpu
from jax.sharding import PartitionSpec as P

epsilon = 1e-05
BF16, F32 = jnp.bfloat16, jnp.float32
VMEM = pl.BlockSpec(memory_space=pltpu.VMEM)
SMEM = pl.BlockSpec(memory_space=pltpu.SMEM)
ANY = pl.BlockSpec(memory_space=pl.ANY)
NT = (((1,), (1,)), ((), ()))
TN = (((0,), (0,)), ((), ()))
ROWS = 16
PITCH = 17
FRONT_ROWS, FRONT_PITCH = 32, 33


FRONT_MIB, PRODUCT_MIB, MIDDLE_MIB, FINISH_MIB = 36, 24, 36, 36


def params(mebibytes):
    return pltpu.CompilerParams(vmem_limit_bytes=mebibytes * 1024 * 1024)


def cost(flops, nbytes, transcendentals=0):
    return pl.CostEstimate(
        flops=int(flops), bytes_accessed=int(nbytes), transcendentals=int(transcendentals)
    )


def normalize(values):
    mean = jnp.mean(values, 0, keepdims=True)
    square = jnp.mean(values * values, 0, keepdims=True)
    return (values - mean) * lax.rsqrt(square - mean * mean + epsilon)


def gated(half_linear, half_gate):
    return half_linear + half_linear * jnp.tanh(half_gate)


def dot(a, b):
    return jnp.dot(a, b, preferred_element_type=F32)


def front_kernel(
    pair_ref, wl_ref, wlg_ref, wr_ref, wrg_ref, out_ref, rows_in, weights_in, spread, sems, w_sems
):
    loads = []
    for step in range(128 // FRONT_ROWS):
        rows = pl.ds(step * FRONT_ROWS, FRONT_ROWS)
        loads.append(
            pltpu.make_async_copy(pair_ref.at[rows], rows_in.at[rows], sems.at[step])
        )
    w_loads = [
        pltpu.make_async_copy(ref.at[0], weights_in.at[pl.ds(64 * n, 64)], w_sems.at[n])
        for n, ref in enumerate((wl_ref, wlg_ref, wr_ref, wrg_ref))
    ]
    for load in w_loads + loads[:2]:
        load.start()
    for load in w_loads:
        load.wait()
    weights = (weights_in[...] * 0.5).astype(BF16)
    group = 4
    for step, load in enumerate(loads):
        load.wait()
        if step + 2 < len(loads):
            loads[step + 2].start()
        start = step * FRONT_ROWS
        for first in range(0, FRONT_ROWS, group):
            state = jnp.concatenate(
                [rows_in[start + first + row].T for row in range(group)], 1
            ).astype(F32)
            linear = dot(weights, normalize(state).astype(BF16))
            left = gated(linear[0:64], linear[64:128])
            right = gated(linear[128:192], linear[192:256])
            for side, tile in enumerate((left, right)):
                for row in range(group):
                    spread[side, pl.ds(first + row, 64, stride=FRONT_PITCH), :] = tile[
                        :, row * 128 : (row + 1) * 128
                    ]
        for side in range(2):
            for c in range(64):
                at = c * FRONT_PITCH
                out_ref[c, side, start : start + FRONT_ROWS] = spread[
                    side, at : at + FRONT_ROWS, :
                ].astype(BF16)


def front(pair, weights):
    return pl.pallas_call(
        front_kernel,
        name="front",
        in_specs=[ANY] * 5,
        out_specs=VMEM,
        out_shape=pltpu.VMEM((64, 2, 128, 128), BF16),
        scratch_shapes=[
            pltpu.VMEM((128, 128, 128), BF16),
            pltpu.VMEM((256, 128), BF16),
            pltpu.VMEM((2, 64 * FRONT_PITCH, 128), F32),
            pltpu.SemaphoreType.DMA((128 // FRONT_ROWS,)),
            pltpu.SemaphoreType.DMA((4,)),
        ],
        compiler_params=params(FRONT_MIB),
        cost_estimate=cost(16384 * 128 * 384 * 2, 12 << 20, 1 << 21),
    )(far(pair), *[far(w) for w in weights])


def turn_kernel(rep_ref, pair_ref, w_ref, state_ref, gate_ref, spread):
    weights = w_ref[...]
    for i in range(128):
        spread[i * FRONT_PITCH : i * FRONT_PITCH + FRONT_ROWS, :] = pair_ref[i].astype(F32)
    group = 4
    for first in range(0, FRONT_ROWS, group):
        state = jnp.concatenate(
            [spread[pl.ds(first + r, 128, stride=FRONT_PITCH), :].T for r in range(group)], 1
        )
        half_gate = dot(weights, normalize(state).astype(BF16))
        where = slice(first * 128, (first + group) * 128)
        state_ref[:, where] = state.astype(BF16)
        gate_ref[:, where] = (0.5 + 0.5 * jnp.tanh(half_gate)).astype(BF16)


def turn(rep, pair, weights):
    steps = 64 // FRONT_ROWS
    return pl.pallas_call(
        turn_kernel,
        name="turn",
        grid_spec=pltpu.PrefetchScalarGridSpec(
            num_scalar_prefetch=1,
            grid=(steps,),
            in_specs=[
                pl.BlockSpec((128, FRONT_ROWS, 128), lambda s, rep: (0, rep[0] * steps + s, 0)),
                pl.BlockSpec((128, 128), lambda s, rep: (0, 0)),
            ],
            out_specs=[pl.BlockSpec((128, FRONT_ROWS * 128), lambda s, rep: (0, s))] * 2,
            scratch_shapes=[pltpu.VMEM((128 * FRONT_PITCH, 128), F32)],
        ),
        out_shape=[pltpu.HBM((128, 8192), BF16)] * 2,
        compiler_params=params(36),
        cost_estimate=cost(8192 * 128 * 256 * 2, 6 << 20, 1 << 20),
    )(rep, pair, weights)


def product_kernel(got_ref, out_ref, *scratch, by_row):
    def block(n, side):
        if by_row:
            return jnp.concatenate([got_ref[n, q, side] for q in range(8)], 1)
        return jnp.concatenate(
            [
                jnp.concatenate([got_ref[p, r, n, side] for r in range(8)], 1)
                for p in range(2)
            ],
            0,
        )

    products = scratch[0] if by_row else out_ref
    copies = []
    for step in range(4):
        left = jnp.concatenate([block(2 * step, 0), block(2 * step + 1, 0)], 0)
        for q in range(0, 8, 2):
            right = jnp.concatenate([block(q, 1), block(q + 1, 1)], 0)
            hidden = lax.dot_general(right, left, NT, preferred_element_type=F32).astype(BF16)
            for qq in range(2):
                for p in range(2):
                    at = qq * 128 + p * 64
                    for r in range(2):
                        products[p, 2 * step + r, q + qq] = hidden[
                            at : at + 64, r * 128 : (r + 1) * 128
                        ]
        for p in range(2 if by_row else 0):
            rows = pl.ds(2 * step, 2)
            copy = pltpu.make_async_copy(
                products.at[p, rows], out_ref.at[p, rows], scratch[1].at[step, p]
            )
            copy.start()
            copies.append(copy)
    for copy in copies:
        copy.wait()


def product(received, by_row):
    out = pl.pallas_call(
        functools.partial(product_kernel, by_row=by_row),
        name="product_out" if by_row else "product_in",
        in_specs=[VMEM],
        out_specs=ANY if by_row else VMEM,
        out_shape=(pltpu.HBM if by_row else pltpu.VMEM)((2, 8, 8, 64, 128), BF16),
        scratch_shapes=[
            pltpu.VMEM((2, 8, 8, 64, 128), BF16),
            pltpu.SemaphoreType.DMA((4, 2)),
        ]
        if by_row
        else [],
        compiler_params=params(PRODUCT_MIB),
        cost_estimate=cost(2 << 30, 6 << 20),
    )(received)
    return out.reshape(128, 64, 128)


def scale_hidden(hidden_ref, first, spread):
    total = jnp.zeros((ROWS, 128), F32)
    squares = jnp.zeros((ROWS, 128), F32)
    for c in range(128):
        values = hidden_ref[c, first : first + ROWS].astype(F32)
        total += values
        squares += values * values
    mean = total * (1.0 / 128)
    factor = lax.rsqrt(squares * (1.0 / 128) - mean * mean + epsilon)
    for c in range(128):
        spread[c * PITCH : c * PITCH + ROWS, :] = (
            hidden_ref[c, first : first + ROWS].astype(F32) - mean
        ) * factor
    return jnp.concatenate(
        [spread[pl.ds(r, 128, stride=PITCH), :] for r in range(ROWS)], 1
    ).astype(BF16)


def both_halves(rep_ref, mine, other):
    first = rep_ref[0] == 0
    return jnp.concatenate(
        [jnp.where(first, mine, other), jnp.where(first, other, mine)], 0
    )


def middle_kernel(
    rep_ref, hidden_ref, state_ref, gate_ref, mine_ref, other_ref, w_gate_ref, new_ref,
    new_gate_ref, out_ref, spread, sides, old_state, old_gate, load_sems,
):
    loads = []
    for first in range(0, 64, ROWS):
        part = pl.ds(first * 128, ROWS * 128)
        loads.append(
            [
                pltpu.make_async_copy(
                    source.at[:, part], target.at[:, part], load_sems.at[n, first // ROWS]
                )
                for n, (source, target) in enumerate(
                    ((state_ref, old_state), (gate_ref, old_gate))
                )
            ]
        )
    for load in loads[0] + loads[1]:
        load.start()
    w_out = both_halves(rep_ref, mine_ref[256:320], other_ref[256:320])
    weights = both_halves(rep_ref, mine_ref[:256], other_ref[:256])
    for first in range(0, 64, ROWS):
        where = slice(first * 128, (first + ROWS) * 128)
        scaled = scale_hidden(hidden_ref, first, spread)
        projected = lax.dot_general(w_out, scaled, TN, preferred_element_type=F32)
        step = first // ROWS
        for load in loads[step]:
            load.wait()
        if step + 2 < len(loads):
            for load in loads[step + 2]:
                load.start()
        state = old_state[:, where].astype(F32) + old_gate[:, where].astype(F32) * projected
        new_ref[:, where] = state.astype(new_ref.dtype)
        normed = normalize(state).astype(BF16)
        half_gate = dot(w_gate_ref[...], normed)
        new_gate_ref[:, where] = (0.5 + 0.5 * jnp.tanh(half_gate)).astype(BF16)
        linear = dot(weights, normed)
        for half in range(2):
            at = half * 256
            left = gated(linear[at : at + 64], linear[at + 64 : at + 128])
            right = gated(linear[at + 128 : at + 192], linear[at + 192 : at + 256])
            for side, tile in enumerate((left, right)):
                for row in range(ROWS):
                    sides[side, pl.ds(half * 64 * PITCH + row, 64, stride=PITCH), :] = tile[
                        :, row * 128 : (row + 1) * 128
                    ]
        for side in range(2):
            for c in range(128):
                out_ref[c, side, first : first + ROWS] = sides[
                    side, c * PITCH : c * PITCH + ROWS, :
                ].astype(BF16)


def middle(rep, hidden, state, gate, mine, other, w_gate):
    return pl.pallas_call(
        middle_kernel,
        name="middle",
        in_specs=[SMEM, VMEM, ANY, ANY, VMEM, VMEM, VMEM],
        out_specs=[VMEM, VMEM, VMEM],
        out_shape=[
            jax.ShapeDtypeStruct((128, 8192), BF16),
            jax.ShapeDtypeStruct((128, 8192), BF16),
            pltpu.VMEM((128, 2, 64, 128), BF16),
        ],
        scratch_shapes=[
            pltpu.VMEM((128 * PITCH, 128), F32),
            pltpu.VMEM((2, 128 * PITCH, 128), F32),
            pltpu.VMEM((128, 8192), BF16),
            pltpu.VMEM((128, 8192), BF16),
            pltpu.SemaphoreType.DMA((2, 64 // ROWS)),
        ],
        compiler_params=params(MIDDLE_MIB),
        cost_estimate=cost(8192 * 128 * 640 * 2, 14 << 20, 1 << 21),
    )(rep, hidden, state, gate, mine, other, w_gate)


def finish_kernel(
    rep_ref, hidden_ref, state_ref, gate_ref, mine_ref, other_ref, w_in_ref, w_down_ref,
    out_ref, spread, state_scr, normed_scr, turned, packed, sems,
):
    w_out = both_halves(rep_ref, mine_ref[320:], other_ref[320:])
    w_half_gate = (w_in_ref[:512] * 0.5).astype(BF16)
    group = 8
    copies = []
    for first in range(0, 64, ROWS):
        where = slice(first * 128, (first + ROWS) * 128)
        scaled = scale_hidden(hidden_ref, first, spread)
        projected = lax.dot_general(w_out, scaled, TN, preferred_element_type=F32)
        state = state_ref[:, where].astype(F32) + gate_ref[:, where].astype(F32) * projected
        state_scr[...] = state
        normed_scr[...] = normalize(state).astype(BF16)
        for start in range(0, ROWS, group):
            part = slice(start * 128, (start + group) * 128)
            normed = normed_scr[:, part]
            half_gate = dot(w_half_gate, normed)
            linear = dot(w_in_ref[512:], normed)
            active = (gated(half_gate, half_gate) * linear).astype(BF16)
            updated = state_scr[:, part] + dot(w_down_ref[...], active)
            for row in range(group):
                turned[pl.ds(start + row, 128, stride=PITCH), :] = updated[
                    :, row * 128 : (row + 1) * 128
                ].T
        for i in range(128):
            packed[i, first : first + ROWS] = turned[i * PITCH : i * PITCH + ROWS, :].astype(
                BF16
            )
        rows = pl.ds(first, ROWS)
        copy = pltpu.make_async_copy(
            packed.at[:, rows], out_ref.at[:, rows], sems.at[first // ROWS]
        )
        copy.start()
        copies.append(copy)
    for copy in copies:
        copy.wait()


def finish(rep, hidden, state, gate, mine, other, w_in, w_down):
    return pl.pallas_call(
        finish_kernel,
        name="finish",
        in_specs=[SMEM] + [VMEM] * 7,
        out_specs=ANY,
        out_shape=pltpu.HBM((128, 64, 128), BF16),
        scratch_shapes=[
            pltpu.VMEM((128 * PITCH, 128), F32),
            pltpu.VMEM((128, ROWS * 128), F32),
            pltpu.VMEM((128, ROWS * 128), BF16),
            pltpu.VMEM((128 * PITCH, 128), F32),
            pltpu.VMEM((128, 64, 128), BF16),
            pltpu.SemaphoreType.DMA((64 // ROWS,)),
        ],
        compiler_params=params(FINISH_MIB),
        cost_estimate=cost(8192 * 128 * 1664 * 2, 10 << 20, 1 << 22),
    )(rep, hidden, state, gate, mine, other, w_in, w_down)


def exchange(values, axes):
    return lax.all_to_all(values, axes, split_axis=0, concat_axis=0, tiled=True)


def near(values):
    return pltpu.with_memory_space_constraint(values, pltpu.VMEM)


def far(values):
    return pltpu.with_memory_space_constraint(values, pltpu.HBM)


def on_device(
    pair, w_left, w_left_gate, w_right, w_right_gate, w_gate, w_out, w_trans_in, w_trans_out
):
    rep = lax.axis_index("rep").astype(jnp.int32).reshape(1)
    everywhere = ("rep", "row", "col")
    projections = [
        w.transpose(0, 2, 1) for w in (w_left, w_left_gate, w_right, w_right_gate)
    ]
    sides = front(pair, projections)
    sides, rep = lax.optimization_barrier((sides, rep))
    received = exchange(sides, ("row", "col"))

    products = product(near(received.reshape(8, 8, 2, 128, 128)), True)
    products, pair, w_gate, w_out, w_trans_in, w_trans_out, *projections = (
        lax.optimization_barrier(
            (products, pair, w_gate, w_out, w_trans_in, w_trans_out, *projections)
        )
    )
    hidden = exchange(products, everywhere)

    mine = jnp.concatenate(
        [(w[1] * 0.5).astype(BF16) for w in projections] + [w_out[0], w_out[1]], 0
    )
    other = lax.ppermute(mine, "rep", [(0, 1), (1, 0)])
    gates = (w_gate * 0.5).astype(BF16).transpose(0, 2, 1)
    w_in = w_trans_in.T
    w_down = w_trans_out.T
    state, gate = turn(rep, pair, gates[0])
    hidden, state, gate, gates, w_in, w_down, mine, other = lax.optimization_barrier(
        (hidden, state, gate, gates, w_in, w_down, mine, other)
    )

    state, gate, sides = middle(rep, near(hidden), far(state), far(gate), mine, other, gates[1])
    received = exchange(sides, everywhere)
    hidden = exchange(product(near(received.reshape(2, 8, 8, 2, 64, 128)), False), everywhere)
    return finish(rep, near(hidden), state, gate, mine, other, w_in, w_down)


def solution(mesh):
    placed = (
        P("row", "col", None),
        P(None, None, "rep"),
        P(None, None, "rep"),
        P(None, None, "rep"),
        P(None, None, "rep"),
        P(),
        P(None, "rep", None),
        P(),
        P(),
    )
    return jax.shard_map(
        on_device,
        mesh=mesh,
        in_specs=placed,
        out_specs=P("row", ("col", "rep"), None),
        check_vma=False,
    )
```

```python
import functools

import jax
import jax.numpy as jnp
from jax import lax
from jax.experimental import pallas as pl
from jax.experimental.pallas import tpu as pltpu
from jax.sharding import PartitionSpec as P

epsilon = 1e-05
BF16, F32 = jnp.bfloat16, jnp.float32
VMEM = pl.BlockSpec(memory_space=pltpu.VMEM)
SMEM = pl.BlockSpec(memory_space=pltpu.SMEM)
ANY = pl.BlockSpec(memory_space=pl.ANY)
NT = (((1,), (1,)), ((), ()))
TN = (((0,), (0,)), ((), ()))
ROWS = 16
PITCH = 17
FRONT_ROWS, FRONT_PITCH = 32, 33


FRONT_MIB, PRODUCT_MIB, MIDDLE_MIB, FINISH_MIB = 36, 24, 36, 36


def params(mebibytes):
    return pltpu.CompilerParams(vmem_limit_bytes=mebibytes * 1024 * 1024)


def cost(flops, nbytes, transcendentals=0):
    return pl.CostEstimate(
        flops=int(flops), bytes_accessed=int(nbytes), transcendentals=int(transcendentals)
    )


def normalize(values):
    mean = jnp.mean(values, 0, keepdims=True)
    square = jnp.mean(values * values, 0, keepdims=True)
    return (values - mean) * lax.rsqrt(square - mean * mean + epsilon)


def gated(half_linear, half_gate):
    return half_linear + half_linear * jnp.tanh(half_gate)


def dot(a, b):
    return jnp.dot(a, b, preferred_element_type=F32)


def front_kernel(
    pair_ref, wl_ref, wlg_ref, wr_ref, wrg_ref, out_ref, rows_in, weights_in, spread, sems, w_sems
):
    loads = []
    for step in range(128 // FRONT_ROWS):
        rows = pl.ds(step * FRONT_ROWS, FRONT_ROWS)
        loads.append(
            pltpu.make_async_copy(pair_ref.at[rows], rows_in.at[rows], sems.at[step])
        )
    w_loads = [
        pltpu.make_async_copy(ref.at[0], weights_in.at[pl.ds(64 * n, 64)], w_sems.at[n])
        for n, ref in enumerate((wl_ref, wlg_ref, wr_ref, wrg_ref))
    ]
    for load in w_loads + loads[:2]:
        load.start()
    for load in w_loads:
        load.wait()
    weights = (weights_in[...] * 0.5).astype(BF16)
    group = 4
    for step, load in enumerate(loads):
        load.wait()
        if step + 2 < len(loads):
            loads[step + 2].start()
        start = step * FRONT_ROWS
        for first in range(0, FRONT_ROWS, group):
            state = jnp.concatenate(
                [rows_in[start + first + row].T for row in range(group)], 1
            ).astype(F32)
            linear = dot(weights, normalize(state).astype(BF16))
            left = gated(linear[0:64], linear[64:128])
            right = gated(linear[128:192], linear[192:256])
            for side, tile in enumerate((left, right)):
                for row in range(group):
                    spread[side, pl.ds(first + row, 64, stride=FRONT_PITCH), :] = tile[
                        :, row * 128 : (row + 1) * 128
                    ]
        for side in range(2):
            for c in range(64):
                at = c * FRONT_PITCH
                out_ref[c, side, start : start + FRONT_ROWS] = spread[
                    side, at : at + FRONT_ROWS, :
                ].astype(BF16)


def front(pair, weights):
    return pl.pallas_call(
        front_kernel,
        name="front",
        in_specs=[ANY] * 5,
        out_specs=VMEM,
        out_shape=pltpu.VMEM((64, 2, 128, 128), BF16),
        scratch_shapes=[
            pltpu.VMEM((128, 128, 128), BF16),
            pltpu.VMEM((256, 128), BF16),
            pltpu.VMEM((2, 64 * FRONT_PITCH, 128), F32),
            pltpu.SemaphoreType.DMA((128 // FRONT_ROWS,)),
            pltpu.SemaphoreType.DMA((4,)),
        ],
        compiler_params=params(FRONT_MIB),
        cost_estimate=cost(16384 * 128 * 384 * 2, 12 << 20, 1 << 21),
    )(far(pair), *[far(w) for w in weights])


def turn_kernel(rep_ref, pair_ref, w_ref, state_ref, gate_ref, spread):
    weights = w_ref[...]
    for i in range(128):
        spread[i * FRONT_PITCH : i * FRONT_PITCH + FRONT_ROWS, :] = pair_ref[i].astype(F32)
    group = 4
    for first in range(0, FRONT_ROWS, group):
        state = jnp.concatenate(
            [spread[pl.ds(first + r, 128, stride=FRONT_PITCH), :].T for r in range(group)], 1
        )
        half_gate = dot(weights, normalize(state).astype(BF16))
        where = slice(first * 128, (first + group) * 128)
        state_ref[:, where] = state.astype(BF16)
        gate_ref[:, where] = (0.5 + 0.5 * jnp.tanh(half_gate)).astype(BF16)


def turn(rep, pair, weights):
    steps = 64 // FRONT_ROWS
    return pl.pallas_call(
        turn_kernel,
        name="turn",
        grid_spec=pltpu.PrefetchScalarGridSpec(
            num_scalar_prefetch=1,
            grid=(steps,),
            in_specs=[
                pl.BlockSpec((128, FRONT_ROWS, 128), lambda s, rep: (0, rep[0] * steps + s, 0)),
                pl.BlockSpec((128, 128), lambda s, rep: (0, 0)),
            ],
            out_specs=[pl.BlockSpec((128, FRONT_ROWS * 128), lambda s, rep: (0, s))] * 2,
            scratch_shapes=[pltpu.VMEM((128 * FRONT_PITCH, 128), F32)],
        ),
        out_shape=[pltpu.HBM((128, 8192), BF16)] * 2,
        compiler_params=params(36),
        cost_estimate=cost(8192 * 128 * 256 * 2, 6 << 20, 1 << 20),
    )(rep, pair, weights)


def product_kernel(got_ref, out_ref, *scratch, by_row):
    def block(n, side):
        if by_row:
            return jnp.concatenate([got_ref[n, q, side] for q in range(8)], 1)
        return jnp.concatenate(
            [
                jnp.concatenate([got_ref[r, p, n, side] for r in range(8)], 1)
                for p in range(2)
            ],
            0,
        )

    products = scratch[0] if by_row else out_ref
    copies = []
    for step in range(4):
        left = jnp.concatenate([block(2 * step, 0), block(2 * step + 1, 0)], 0)
        for q in range(0, 8, 2):
            right = jnp.concatenate([block(q, 1), block(q + 1, 1)], 0)
            hidden = lax.dot_general(right, left, NT, preferred_element_type=F32).astype(BF16)
            for qq in range(2):
                for p in range(2):
                    at = qq * 128 + p * 64
                    for r in range(2):
                        products[2 * step + r, p, q + qq] = hidden[
                            at : at + 64, r * 128 : (r + 1) * 128
                        ]
        if by_row:
            rows = pl.ds(2 * step, 2)
            copy = pltpu.make_async_copy(
                products.at[rows], out_ref.at[rows], scratch[1].at[step]
            )
            copy.start()
            copies.append(copy)
    for copy in copies:
        copy.wait()


def product(received, by_row):
    out = pl.pallas_call(
        functools.partial(product_kernel, by_row=by_row),
        name="product_out" if by_row else "product_in",
        in_specs=[VMEM],
        out_specs=ANY if by_row else VMEM,
        out_shape=(pltpu.HBM if by_row else pltpu.VMEM)((8, 2, 8, 64, 128), BF16),
        scratch_shapes=[
            pltpu.VMEM((8, 2, 8, 64, 128), BF16),
            pltpu.SemaphoreType.DMA((4,)),
        ]
        if by_row
        else [],
        compiler_params=params(PRODUCT_MIB),
        cost_estimate=cost(2 << 30, 6 << 20),
    )(received)
    return out.reshape(128, 64, 128)


def scale_hidden(hidden_ref, first, spread):
    total = jnp.zeros((ROWS, 128), F32)
    squares = jnp.zeros((ROWS, 128), F32)
    for c in range(128):
        values = hidden_ref[c, first : first + ROWS].astype(F32)
        total += values
        squares += values * values
    mean = total * (1.0 / 128)
    factor = lax.rsqrt(squares * (1.0 / 128) - mean * mean + epsilon)
    for c in range(128):
        spread[c * PITCH : c * PITCH + ROWS, :] = (
            hidden_ref[c, first : first + ROWS].astype(F32) - mean
        ) * factor
    return jnp.concatenate(
        [spread[pl.ds(r, 128, stride=PITCH), :] for r in range(ROWS)], 1
    ).astype(BF16)


def both_halves(rep_ref, mine, other):
    first = rep_ref[0] == 0
    return jnp.concatenate(
        [jnp.where(first, mine, other), jnp.where(first, other, mine)], 0
    )


def by_source(weights):
    rows = weights.astype(F32)
    return jnp.concatenate(
        [rows[p * 64 + r * 8 : p * 64 + r * 8 + 8] for r in range(8) for p in range(2)], 0
    ).astype(BF16)


def middle_kernel(
    rep_ref, hidden_ref, state_ref, gate_ref, mine_ref, other_ref, w_gate_ref, new_ref,
    new_gate_ref, out_ref, spread, sides, old_state, old_gate, load_sems,
):
    loads = []
    for first in range(0, 64, ROWS):
        part = pl.ds(first * 128, ROWS * 128)
        loads.append(
            [
                pltpu.make_async_copy(
                    source.at[:, part], target.at[:, part], load_sems.at[n, first // ROWS]
                )
                for n, (source, target) in enumerate(
                    ((state_ref, old_state), (gate_ref, old_gate))
                )
            ]
        )
    for load in loads[0] + loads[1]:
        load.start()
    w_out = by_source(both_halves(rep_ref, mine_ref[256:320], other_ref[256:320]))
    weights = both_halves(rep_ref, mine_ref[:256], other_ref[:256])
    for first in range(0, 64, ROWS):
        where = slice(first * 128, (first + ROWS) * 128)
        scaled = scale_hidden(hidden_ref, first, spread)
        projected = lax.dot_general(w_out, scaled, TN, preferred_element_type=F32)
        step = first // ROWS
        for load in loads[step]:
            load.wait()
        if step + 2 < len(loads):
            for load in loads[step + 2]:
                load.start()
        state = old_state[:, where].astype(F32) + old_gate[:, where].astype(F32) * projected
        new_ref[:, where] = state.astype(new_ref.dtype)
        normed = normalize(state).astype(BF16)
        half_gate = dot(w_gate_ref[...], normed)
        new_gate_ref[:, where] = (0.5 + 0.5 * jnp.tanh(half_gate)).astype(BF16)
        linear = dot(weights, normed)
        for half in range(2):
            at = half * 256
            left = gated(linear[at : at + 64], linear[at + 64 : at + 128])
            right = gated(linear[at + 128 : at + 192], linear[at + 192 : at + 256])
            for side, tile in enumerate((left, right)):
                for row in range(ROWS):
                    sides[side, pl.ds(half * 64 * PITCH + row, 64, stride=PITCH), :] = tile[
                        :, row * 128 : (row + 1) * 128
                    ]
        for side in range(2):
            for c in range(128):
                out_ref[c, side, first : first + ROWS] = sides[
                    side, c * PITCH : c * PITCH + ROWS, :
                ].astype(BF16)


def middle(rep, hidden, state, gate, mine, other, w_gate):
    return pl.pallas_call(
        middle_kernel,
        name="middle",
        in_specs=[SMEM, VMEM, ANY, ANY, VMEM, VMEM, VMEM],
        out_specs=[VMEM, VMEM, VMEM],
        out_shape=[
            jax.ShapeDtypeStruct((128, 8192), BF16),
            jax.ShapeDtypeStruct((128, 8192), BF16),
            pltpu.VMEM((128, 2, 64, 128), BF16),
        ],
        scratch_shapes=[
            pltpu.VMEM((128 * PITCH, 128), F32),
            pltpu.VMEM((2, 128 * PITCH, 128), F32),
            pltpu.VMEM((128, 8192), BF16),
            pltpu.VMEM((128, 8192), BF16),
            pltpu.SemaphoreType.DMA((2, 64 // ROWS)),
        ],
        compiler_params=params(MIDDLE_MIB),
        cost_estimate=cost(8192 * 128 * 640 * 2, 14 << 20, 1 << 21),
    )(rep, hidden, state, gate, mine, other, w_gate)


def finish_kernel(
    rep_ref, hidden_ref, state_ref, gate_ref, mine_ref, other_ref, w_in_ref, w_down_ref,
    out_ref, spread, state_scr, normed_scr, turned, packed, sems,
):
    w_out = both_halves(rep_ref, mine_ref[320:], other_ref[320:])
    w_half_gate = (w_in_ref[:512] * 0.5).astype(BF16)
    group = 8
    copies = []
    for first in range(0, 64, ROWS):
        where = slice(first * 128, (first + ROWS) * 128)
        scaled = scale_hidden(hidden_ref, first, spread)
        projected = lax.dot_general(w_out, scaled, TN, preferred_element_type=F32)
        state = state_ref[:, where].astype(F32) + gate_ref[:, where].astype(F32) * projected
        state_scr[...] = state
        normed_scr[...] = normalize(state).astype(BF16)
        for start in range(0, ROWS, group):
            part = slice(start * 128, (start + group) * 128)
            normed = normed_scr[:, part]
            half_gate = dot(w_half_gate, normed)
            linear = dot(w_in_ref[512:], normed)
            active = (gated(half_gate, half_gate) * linear).astype(BF16)
            updated = state_scr[:, part] + dot(w_down_ref[...], active)
            for row in range(group):
                turned[pl.ds(start + row, 128, stride=PITCH), :] = updated[
                    :, row * 128 : (row + 1) * 128
                ].T
        for i in range(128):
            packed[i, first : first + ROWS] = turned[i * PITCH : i * PITCH + ROWS, :].astype(
                BF16
            )
        rows = pl.ds(first, ROWS)
        copy = pltpu.make_async_copy(
            packed.at[:, rows], out_ref.at[:, rows], sems.at[first // ROWS]
        )
        copy.start()
        copies.append(copy)
    for copy in copies:
        copy.wait()


def finish(rep, hidden, state, gate, mine, other, w_in, w_down):
    return pl.pallas_call(
        finish_kernel,
        name="finish",
        in_specs=[SMEM] + [VMEM] * 7,
        out_specs=ANY,
        out_shape=pltpu.HBM((128, 64, 128), BF16),
        scratch_shapes=[
            pltpu.VMEM((128 * PITCH, 128), F32),
            pltpu.VMEM((128, ROWS * 128), F32),
            pltpu.VMEM((128, ROWS * 128), BF16),
            pltpu.VMEM((128 * PITCH, 128), F32),
            pltpu.VMEM((128, 64, 128), BF16),
            pltpu.SemaphoreType.DMA((64 // ROWS,)),
        ],
        compiler_params=params(FINISH_MIB),
        cost_estimate=cost(8192 * 128 * 1664 * 2, 10 << 20, 1 << 22),
    )(rep, hidden, state, gate, mine, other, w_in, w_down)


def exchange(values, axes):
    return lax.all_to_all(values, axes, split_axis=0, concat_axis=0, tiled=True)


def near(values):
    return pltpu.with_memory_space_constraint(values, pltpu.VMEM)


def far(values):
    return pltpu.with_memory_space_constraint(values, pltpu.HBM)


def on_device(
    pair, w_left, w_left_gate, w_right, w_right_gate, w_gate, w_out, w_trans_in, w_trans_out
):
    rep = lax.axis_index("rep").astype(jnp.int32).reshape(1)
    everywhere = ("row", "rep", "col")
    projections = [
        w.transpose(0, 2, 1) for w in (w_left, w_left_gate, w_right, w_right_gate)
    ]
    sides = front(pair, projections)
    sides, rep = lax.optimization_barrier((sides, rep))
    received = exchange(sides, ("row", "col"))

    products = product(near(received.reshape(8, 8, 2, 128, 128)), True)
    products, pair, w_gate, w_out, w_trans_in, w_trans_out, *projections = (
        lax.optimization_barrier(
            (products, pair, w_gate, w_out, w_trans_in, w_trans_out, *projections)
        )
    )
    hidden = exchange(products, everywhere)

    mine = jnp.concatenate(
        [(w[1] * 0.5).astype(BF16) for w in projections] + [w_out[0], w_out[1]], 0
    )
    other = lax.ppermute(mine, "rep", [(0, 1), (1, 0)])
    gates = (w_gate * 0.5).astype(BF16).transpose(0, 2, 1)
    w_in = w_trans_in.T
    w_down = w_trans_out.T
    state, gate = turn(rep, pair, gates[0])
    hidden, state, gate, gates, w_in, w_down, mine, other = lax.optimization_barrier(
        (hidden, state, gate, gates, w_in, w_down, mine, other)
    )

    state, gate, sides = middle(rep, near(hidden), far(state), far(gate), mine, other, gates[1])
    received = exchange(sides, everywhere)
    hidden = exchange(product(near(received.reshape(8, 2, 8, 2, 64, 128)), False), everywhere)
    return finish(rep, near(hidden), state, gate, mine, other, w_in, w_down)


def solution(mesh):
    placed = (
        P("row", "col", None),
        P(None, None, "rep"),
        P(None, None, "rep"),
        P(None, None, "rep"),
        P(None, None, "rep"),
        P(),
        P(None, "rep", None),
        P(),
        P(),
    )
    return jax.shard_map(
        on_device,
        mesh=mesh,
        in_specs=placed,
        out_specs=P("row", ("col", "rep"), None),
        check_vma=False,
    )
```

```python
import functools

import jax
import jax.numpy as jnp
from jax import lax
from jax.experimental import pallas as pl
from jax.experimental.pallas import tpu as pltpu
from jax.sharding import PartitionSpec as P

epsilon = 1e-05
BF16, F32 = jnp.bfloat16, jnp.float32
VMEM = pl.BlockSpec(memory_space=pltpu.VMEM)
SMEM = pl.BlockSpec(memory_space=pltpu.SMEM)
ANY = pl.BlockSpec(memory_space=pl.ANY)
NT = (((1,), (1,)), ((), ()))
TN = (((0,), (0,)), ((), ()))
ROWS = 16
PITCH = 17
FRONT_ROWS, FRONT_PITCH = 32, 33


FRONT_MIB, PRODUCT_MIB, MIDDLE_MIB, FINISH_MIB = 36, 24, 36, 36


def params(mebibytes):
    return pltpu.CompilerParams(vmem_limit_bytes=mebibytes * 1024 * 1024)


def cost(flops, nbytes, transcendentals=0):
    return pl.CostEstimate(
        flops=int(flops), bytes_accessed=int(nbytes), transcendentals=int(transcendentals)
    )


def normalize(values):
    mean = jnp.mean(values, 0, keepdims=True)
    square = jnp.mean(values * values, 0, keepdims=True)
    return (values - mean) * lax.rsqrt(square - mean * mean + epsilon)


def gated(half_linear, half_gate):
    return half_linear + half_linear * jnp.tanh(half_gate)


def dot(a, b):
    return jnp.dot(a, b, preferred_element_type=F32)


def front_kernel(
    pair_ref, wl_ref, wlg_ref, wr_ref, wrg_ref, out_ref, rows_in, weights_in, spread, sems, w_sems
):
    loads = []
    for step in range(128 // FRONT_ROWS):
        rows = pl.ds(step * FRONT_ROWS, FRONT_ROWS)
        loads.append(
            pltpu.make_async_copy(pair_ref.at[rows], rows_in.at[rows], sems.at[step])
        )
    w_loads = [
        pltpu.make_async_copy(ref.at[0], weights_in.at[pl.ds(64 * n, 64)], w_sems.at[n])
        for n, ref in enumerate((wl_ref, wlg_ref, wr_ref, wrg_ref))
    ]
    for load in w_loads + loads[:2]:
        load.start()
    for load in w_loads:
        load.wait()
    weights = (weights_in[...] * 0.5).astype(BF16)
    group = 4
    for step, load in enumerate(loads):
        load.wait()
        if step + 2 < len(loads):
            loads[step + 2].start()
        start = step * FRONT_ROWS
        for first in range(0, FRONT_ROWS, group):
            state = jnp.concatenate(
                [rows_in[start + first + row].T for row in range(group)], 1
            ).astype(F32)
            linear = dot(weights, normalize(state).astype(BF16))
            left = gated(linear[0:64], linear[64:128])
            right = gated(linear[128:192], linear[192:256])
            for side, tile in enumerate((left, right)):
                for row in range(group):
                    spread[side, pl.ds(first + row, 64, stride=FRONT_PITCH), :] = tile[
                        :, row * 128 : (row + 1) * 128
                    ]
        for side in range(2):
            for c in range(64):
                at = c * FRONT_PITCH
                out_ref[c, side, start : start + FRONT_ROWS] = spread[
                    side, at : at + FRONT_ROWS, :
                ].astype(BF16)


def front(pair, weights):
    return pl.pallas_call(
        front_kernel,
        name="front",
        in_specs=[ANY] * 5,
        out_specs=VMEM,
        out_shape=pltpu.VMEM((64, 2, 128, 128), BF16),
        scratch_shapes=[
            pltpu.VMEM((128, 128, 128), BF16),
            pltpu.VMEM((256, 128), BF16),
            pltpu.VMEM((2, 65 * FRONT_PITCH, 128), F32),
            pltpu.SemaphoreType.DMA((128 // FRONT_ROWS,)),
            pltpu.SemaphoreType.DMA((4,)),
        ],
        compiler_params=params(FRONT_MIB),
        cost_estimate=cost(16384 * 128 * 384 * 2, 12 << 20, 1 << 21),
    )(far(pair), *[far(w) for w in weights])


def turn_kernel(rep_ref, pair_ref, w_ref, state_ref, gate_ref, spread):
    weights = w_ref[...]
    for i in range(128):
        spread[i * FRONT_PITCH : i * FRONT_PITCH + FRONT_ROWS, :] = pair_ref[i].astype(F32)
    group = 4
    for first in range(0, FRONT_ROWS, group):
        state = jnp.concatenate(
            [spread[pl.ds(first + r, 128, stride=FRONT_PITCH), :].T for r in range(group)], 1
        )
        half_gate = dot(weights, normalize(state).astype(BF16))
        where = slice(first * 128, (first + group) * 128)
        state_ref[:, where] = state.astype(BF16)
        gate_ref[:, where] = (0.5 + 0.5 * jnp.tanh(half_gate)).astype(BF16)


def turn(rep, pair, weights):
    steps = 64 // FRONT_ROWS
    return pl.pallas_call(
        turn_kernel,
        name="turn",
        grid_spec=pltpu.PrefetchScalarGridSpec(
            num_scalar_prefetch=1,
            grid=(steps,),
            in_specs=[
                pl.BlockSpec((128, FRONT_ROWS, 128), lambda s, rep: (0, rep[0] * steps + s, 0)),
                pl.BlockSpec((128, 128), lambda s, rep: (0, 0)),
            ],
            out_specs=[pl.BlockSpec((128, FRONT_ROWS * 128), lambda s, rep: (0, s))] * 2,
            scratch_shapes=[pltpu.VMEM((129 * FRONT_PITCH, 128), F32)],
        ),
        out_shape=[pltpu.HBM((128, 8192), BF16)] * 2,
        compiler_params=params(36),
        cost_estimate=cost(8192 * 128 * 256 * 2, 6 << 20, 1 << 20),
    )(rep, pair, weights)


def product_kernel(got_ref, out_ref, *scratch, by_row):
    def block(n, side):
        if by_row:
            return jnp.concatenate([got_ref[n, q, side] for q in range(8)], 1)
        return jnp.concatenate(
            [
                jnp.concatenate([got_ref[r, p, n, side] for r in range(8)], 1)
                for p in range(2)
            ],
            0,
        )

    products = scratch[0] if by_row else out_ref
    copies = []
    for step in range(4):
        left = jnp.concatenate([block(2 * step, 0), block(2 * step + 1, 0)], 0)
        for q in range(0, 8, 2):
            right = jnp.concatenate([block(q, 1), block(q + 1, 1)], 0)
            hidden = lax.dot_general(right, left, NT, preferred_element_type=F32).astype(BF16)
            for qq in range(2):
                for p in range(2):
                    at = qq * 128 + p * 64
                    for r in range(2):
                        products[2 * step + r, p, q + qq] = hidden[
                            at : at + 64, r * 128 : (r + 1) * 128
                        ]
        if by_row:
            rows = pl.ds(2 * step, 2)
            copy = pltpu.make_async_copy(
                products.at[rows], out_ref.at[rows], scratch[1].at[step]
            )
            copy.start()
            copies.append(copy)
    for copy in copies:
        copy.wait()


def product(received, by_row):
    out = pl.pallas_call(
        functools.partial(product_kernel, by_row=by_row),
        name="product_out" if by_row else "product_in",
        in_specs=[VMEM],
        out_specs=ANY if by_row else VMEM,
        out_shape=(pltpu.HBM if by_row else pltpu.VMEM)((8, 2, 8, 64, 128), BF16),
        scratch_shapes=[
            pltpu.VMEM((8, 2, 8, 64, 128), BF16),
            pltpu.SemaphoreType.DMA((4,)),
        ]
        if by_row
        else [],
        compiler_params=params(PRODUCT_MIB),
        cost_estimate=cost(2 << 30, 6 << 20),
    )(received)
    return out.reshape(128, 64, 128)


def scale_hidden(hidden_ref, first, spread):
    total = jnp.zeros((ROWS, 128), F32)
    squares = jnp.zeros((ROWS, 128), F32)
    for c in range(128):
        values = hidden_ref[c, first : first + ROWS].astype(F32)
        total += values
        squares += values * values
    mean = total * (1.0 / 128)
    factor = lax.rsqrt(squares * (1.0 / 128) - mean * mean + epsilon)
    for c in range(128):
        spread[c * PITCH : c * PITCH + ROWS, :] = (
            hidden_ref[c, first : first + ROWS].astype(F32) - mean
        ) * factor
    return jnp.concatenate(
        [spread[pl.ds(r, 128, stride=PITCH), :] for r in range(ROWS)], 1
    ).astype(BF16)


def both_halves(rep_ref, mine, other):
    first = rep_ref[0] == 0
    return jnp.concatenate(
        [jnp.where(first, mine, other), jnp.where(first, other, mine)], 0
    )


def by_source(weights):
    rows = weights.astype(F32)
    return jnp.concatenate(
        [rows[p * 64 + r * 8 : p * 64 + r * 8 + 8] for r in range(8) for p in range(2)], 0
    ).astype(BF16)


def middle_kernel(
    rep_ref, hidden_ref, state_ref, gate_ref, mine_ref, other_ref, w_gate_ref, new_ref,
    new_gate_ref, out_ref, spread, sides, old_state, old_gate, load_sems,
):
    loads = []
    for first in range(0, 64, ROWS):
        part = pl.ds(first * 128, ROWS * 128)
        loads.append(
            [
                pltpu.make_async_copy(
                    source.at[:, part], target.at[:, part], load_sems.at[n, first // ROWS]
                )
                for n, (source, target) in enumerate(
                    ((state_ref, old_state), (gate_ref, old_gate))
                )
            ]
        )
    for load in loads[0] + loads[1]:
        load.start()
    w_out = by_source(both_halves(rep_ref, mine_ref[256:320], other_ref[256:320]))
    weights = both_halves(rep_ref, mine_ref[:256], other_ref[:256])
    for first in range(0, 64, ROWS):
        where = slice(first * 128, (first + ROWS) * 128)
        scaled = scale_hidden(hidden_ref, first, spread)
        projected = lax.dot_general(w_out, scaled, TN, preferred_element_type=F32)
        step = first // ROWS
        for load in loads[step]:
            load.wait()
        if step + 2 < len(loads):
            for load in loads[step + 2]:
                load.start()
        state = old_state[:, where].astype(F32) + old_gate[:, where].astype(F32) * projected
        new_ref[:, where] = state.astype(new_ref.dtype)
        normed = normalize(state).astype(BF16)
        half_gate = dot(w_gate_ref[...], normed)
        new_gate_ref[:, where] = (0.5 + 0.5 * jnp.tanh(half_gate)).astype(BF16)
        linear = dot(weights, normed)
        for half in range(2):
            at = half * 256
            left = gated(linear[at : at + 64], linear[at + 64 : at + 128])
            right = gated(linear[at + 128 : at + 192], linear[at + 192 : at + 256])
            for side, tile in enumerate((left, right)):
                for row in range(ROWS):
                    sides[side, pl.ds(half * 64 * PITCH + row, 64, stride=PITCH), :] = tile[
                        :, row * 128 : (row + 1) * 128
                    ]
        for side in range(2):
            for c in range(128):
                out_ref[c, side, first : first + ROWS] = sides[
                    side, c * PITCH : c * PITCH + ROWS, :
                ].astype(BF16)


def middle(rep, hidden, state, gate, mine, other, w_gate):
    return pl.pallas_call(
        middle_kernel,
        name="middle",
        in_specs=[SMEM, VMEM, ANY, ANY, VMEM, VMEM, VMEM],
        out_specs=[VMEM, VMEM, VMEM],
        out_shape=[
            jax.ShapeDtypeStruct((128, 8192), BF16),
            jax.ShapeDtypeStruct((128, 8192), BF16),
            pltpu.VMEM((128, 2, 64, 128), BF16),
        ],
        scratch_shapes=[
            pltpu.VMEM((129 * PITCH, 128), F32),
            pltpu.VMEM((2, 129 * PITCH, 128), F32),
            pltpu.VMEM((128, 8192), BF16),
            pltpu.VMEM((128, 8192), BF16),
            pltpu.SemaphoreType.DMA((2, 64 // ROWS)),
        ],
        compiler_params=params(MIDDLE_MIB),
        cost_estimate=cost(8192 * 128 * 640 * 2, 14 << 20, 1 << 21),
    )(rep, hidden, state, gate, mine, other, w_gate)


def finish_kernel(
    rep_ref, hidden_ref, state_ref, gate_ref, mine_ref, other_ref, w_in_ref, w_down_ref,
    out_ref, spread, state_scr, normed_scr, turned, packed, sems,
):
    w_out = both_halves(rep_ref, mine_ref[320:], other_ref[320:])
    w_half_gate = (w_in_ref[:512] * 0.5).astype(BF16)
    group = 8
    copies = []
    for first in range(0, 64, ROWS):
        where = slice(first * 128, (first + ROWS) * 128)
        scaled = scale_hidden(hidden_ref, first, spread)
        projected = lax.dot_general(w_out, scaled, TN, preferred_element_type=F32)
        state = state_ref[:, where].astype(F32) + gate_ref[:, where].astype(F32) * projected
        state_scr[...] = state
        normed_scr[...] = normalize(state).astype(BF16)
        for start in range(0, ROWS, group):
            part = slice(start * 128, (start + group) * 128)
            normed = normed_scr[:, part]
            half_gate = dot(w_half_gate, normed)
            linear = dot(w_in_ref[512:], normed)
            active = (gated(half_gate, half_gate) * linear).astype(BF16)
            updated = state_scr[:, part] + dot(w_down_ref[...], active)
            for row in range(group):
                turned[pl.ds(start + row, 128, stride=PITCH), :] = updated[
                    :, row * 128 : (row + 1) * 128
                ].T
        for i in range(128):
            packed[i, first : first + ROWS] = turned[i * PITCH : i * PITCH + ROWS, :].astype(
                BF16
            )
        rows = pl.ds(first, ROWS)
        copy = pltpu.make_async_copy(
            packed.at[:, rows], out_ref.at[:, rows], sems.at[first // ROWS]
        )
        copy.start()
        copies.append(copy)
    for copy in copies:
        copy.wait()


def finish(rep, hidden, state, gate, mine, other, w_in, w_down):
    return pl.pallas_call(
        finish_kernel,
        name="finish",
        in_specs=[SMEM] + [VMEM] * 7,
        out_specs=ANY,
        out_shape=pltpu.HBM((128, 64, 128), BF16),
        scratch_shapes=[
            pltpu.VMEM((129 * PITCH, 128), F32),
            pltpu.VMEM((128, ROWS * 128), F32),
            pltpu.VMEM((128, ROWS * 128), BF16),
            pltpu.VMEM((129 * PITCH, 128), F32),
            pltpu.VMEM((128, 64, 128), BF16),
            pltpu.SemaphoreType.DMA((64 // ROWS,)),
        ],
        compiler_params=params(FINISH_MIB),
        cost_estimate=cost(8192 * 128 * 1664 * 2, 10 << 20, 1 << 22),
    )(rep, hidden, state, gate, mine, other, w_in, w_down)


def exchange(values, axes):
    return lax.all_to_all(values, axes, split_axis=0, concat_axis=0, tiled=True)


def near(values):
    return pltpu.with_memory_space_constraint(values, pltpu.VMEM)


def far(values):
    return pltpu.with_memory_space_constraint(values, pltpu.HBM)


def on_device(
    pair, w_left, w_left_gate, w_right, w_right_gate, w_gate, w_out, w_trans_in, w_trans_out
):
    rep = lax.axis_index("rep").astype(jnp.int32).reshape(1)
    everywhere = ("row", "rep", "col")
    projections = [
        w.transpose(0, 2, 1) for w in (w_left, w_left_gate, w_right, w_right_gate)
    ]
    sides = front(pair, projections)
    sides, rep = lax.optimization_barrier((sides, rep))
    received = exchange(sides, ("row", "col"))

    products = product(near(received.reshape(8, 8, 2, 128, 128)), True)
    products, pair, w_gate, w_out, w_trans_in, w_trans_out, *projections = (
        lax.optimization_barrier(
            (products, pair, w_gate, w_out, w_trans_in, w_trans_out, *projections)
        )
    )
    hidden = exchange(products, everywhere)

    mine = jnp.concatenate(
        [(w[1] * 0.5).astype(BF16) for w in projections] + [w_out[0], w_out[1]], 0
    )
    other = lax.ppermute(mine, "rep", [(0, 1), (1, 0)])
    gates = (w_gate * 0.5).astype(BF16).transpose(0, 2, 1)
    w_in = w_trans_in.T
    w_down = w_trans_out.T
    state, gate = turn(rep, pair, gates[0])
    hidden, state, gate, gates, w_in, w_down, mine, other = lax.optimization_barrier(
        (hidden, state, gate, gates, w_in, w_down, mine, other)
    )

    state, gate, sides = middle(rep, near(hidden), far(state), far(gate), mine, other, gates[1])
    received = exchange(sides, everywhere)
    hidden = exchange(product(near(received.reshape(8, 2, 8, 2, 64, 128)), False), everywhere)
    return finish(rep, near(hidden), state, gate, mine, other, w_in, w_down)


def solution(mesh):
    placed = (
        P("row", "col", None),
        P(None, None, "rep"),
        P(None, None, "rep"),
        P(None, None, "rep"),
        P(None, None, "rep"),
        P(),
        P(None, "rep", None),
        P(),
        P(),
    )
    return jax.shard_map(
        on_device,
        mesh=mesh,
        in_specs=placed,
        out_specs=P("row", ("col", "rep"), None),
        check_vma=False,
    )
```

```python
import functools

import jax
import jax.numpy as jnp
from jax import lax
from jax.experimental import pallas as pl
from jax.experimental.pallas import tpu as pltpu
from jax.sharding import PartitionSpec as P

epsilon = 1e-05
BF16, F32 = jnp.bfloat16, jnp.float32
VMEM = pl.BlockSpec(memory_space=pltpu.VMEM)
SMEM = pl.BlockSpec(memory_space=pltpu.SMEM)
ANY = pl.BlockSpec(memory_space=pl.ANY)
NT = (((1,), (1,)), ((), ()))
TN = (((0,), (0,)), ((), ()))
ROWS = 16
PITCH = 17
FRONT_ROWS, FRONT_PITCH = 32, 33


FRONT_MIB, PRODUCT_MIB, MIDDLE_MIB, FINISH_MIB = 36, 24, 36, 36


def params(mebibytes):
    return pltpu.CompilerParams(vmem_limit_bytes=mebibytes * 1024 * 1024)


def cost(flops, nbytes, transcendentals=0):
    return pl.CostEstimate(
        flops=int(flops), bytes_accessed=int(nbytes), transcendentals=int(transcendentals)
    )


def normalize(values):
    mean = jnp.mean(values, 0, keepdims=True)
    square = jnp.mean(values * values, 0, keepdims=True)
    return (values - mean) * lax.rsqrt(square - mean * mean + epsilon)


def gated(half_linear, half_gate):
    return half_linear + half_linear * jnp.tanh(half_gate)


def dot(a, b):
    return jnp.dot(a, b, preferred_element_type=F32)


def front_kernel(
    pair_ref, wl_ref, wlg_ref, wr_ref, wrg_ref, out_ref, rows_in, weights_in, spread, sems, w_sems
):
    loads = []
    for step in range(128 // FRONT_ROWS):
        rows = pl.ds(step * FRONT_ROWS, FRONT_ROWS)
        loads.append(
            pltpu.make_async_copy(pair_ref.at[rows], rows_in.at[rows], sems.at[step])
        )
    w_loads = [
        pltpu.make_async_copy(ref.at[0], weights_in.at[pl.ds(64 * n, 64)], w_sems.at[n])
        for n, ref in enumerate((wl_ref, wlg_ref, wr_ref, wrg_ref))
    ]
    for load in w_loads + loads[:2]:
        load.start()
    for load in w_loads:
        load.wait()
    weights = (weights_in[...] * 0.5).astype(BF16)
    group = 4
    for step, load in enumerate(loads):
        load.wait()
        if step + 2 < len(loads):
            loads[step + 2].start()
        start = step * FRONT_ROWS
        for first in range(0, FRONT_ROWS, group):
            state = jnp.concatenate(
                [rows_in[start + first + row].T for row in range(group)], 1
            ).astype(F32)
            linear = dot(weights, normalize(state).astype(BF16))
            left = gated(linear[0:64], linear[64:128])
            right = gated(linear[128:192], linear[192:256])
            for side, tile in enumerate((left, right)):
                for row in range(group):
                    spread[side, pl.ds(first + row, 64, stride=FRONT_PITCH), :] = tile[
                        :, row * 128 : (row + 1) * 128
                    ]
        for side in range(2):
            for c in range(64):
                at = c * FRONT_PITCH
                out_ref[c, side, start : start + FRONT_ROWS] = spread[
                    side, at : at + FRONT_ROWS, :
                ].astype(BF16)


def front(pair, weights):
    return pl.pallas_call(
        front_kernel,
        name="front",
        in_specs=[ANY] * 5,
        out_specs=VMEM,
        out_shape=pltpu.VMEM((64, 2, 128, 128), BF16),
        scratch_shapes=[
            pltpu.VMEM((128, 128, 128), BF16),
            pltpu.VMEM((256, 128), BF16),
            pltpu.VMEM((2, 65 * FRONT_PITCH, 128), F32),
            pltpu.SemaphoreType.DMA((128 // FRONT_ROWS,)),
            pltpu.SemaphoreType.DMA((4,)),
        ],
        compiler_params=params(FRONT_MIB),
        cost_estimate=cost(16384 * 128 * 384 * 2, 12 << 20, 1 << 21),
    )(far(pair), *[far(w) for w in weights])


def turn_kernel(rep_ref, pair_ref, w_ref, state_ref, gate_ref, spread):
    weights = w_ref[...]
    for i in range(128):
        spread[i * FRONT_PITCH : i * FRONT_PITCH + FRONT_ROWS, :] = pair_ref[i].astype(F32)
    group = 4
    for first in range(0, FRONT_ROWS, group):
        state = jnp.concatenate(
            [spread[pl.ds(first + r, 128, stride=FRONT_PITCH), :].T for r in range(group)], 1
        )
        half_gate = dot(weights, normalize(state).astype(BF16))
        where = slice(first * 128, (first + group) * 128)
        state_ref[:, where] = state.astype(BF16)
        gate_ref[:, where] = (0.5 + 0.5 * jnp.tanh(half_gate)).astype(BF16)


def turn(rep, pair, weights):
    steps = 64 // FRONT_ROWS
    return pl.pallas_call(
        turn_kernel,
        name="turn",
        grid_spec=pltpu.PrefetchScalarGridSpec(
            num_scalar_prefetch=1,
            grid=(steps,),
            in_specs=[
                pl.BlockSpec((128, FRONT_ROWS, 128), lambda s, rep: (0, rep[0] * steps + s, 0)),
                pl.BlockSpec((128, 128), lambda s, rep: (0, 0)),
            ],
            out_specs=[pl.BlockSpec((128, FRONT_ROWS * 128), lambda s, rep: (0, s))] * 2,
            scratch_shapes=[pltpu.VMEM((129 * FRONT_PITCH, 128), F32)],
        ),
        out_shape=[pltpu.HBM((128, 8192), BF16)] * 2,
        compiler_params=params(36),
        cost_estimate=cost(8192 * 128 * 256 * 2, 6 << 20, 1 << 20),
    )(rep, pair, weights)


def product_kernel(got_ref, out_ref, *scratch, by_row):
    def block(n, side):
        if by_row:
            return jnp.concatenate([got_ref[n, q, side] for q in range(8)], 1)
        return jnp.concatenate(
            [
                jnp.concatenate([got_ref[r, p, n, side] for r in range(8)], 1)
                for p in range(2)
            ],
            0,
        )

    products = scratch[0] if by_row else out_ref
    copies = []
    for step in range(4):
        left = jnp.concatenate([block(2 * step, 0), block(2 * step + 1, 0)], 0)
        for q in range(0, 8, 2):
            right = jnp.concatenate([block(q, 1), block(q + 1, 1)], 0)
            hidden = lax.dot_general(right, left, NT, preferred_element_type=F32).astype(BF16)
            for qq in range(2):
                for p in range(2):
                    at = qq * 128 + p * 64
                    for r in range(2):
                        products[2 * step + r, p, q + qq] = hidden[
                            at : at + 64, r * 128 : (r + 1) * 128
                        ]
        if by_row:
            rows = pl.ds(2 * step, 2)
            copy = pltpu.make_async_copy(
                products.at[rows], out_ref.at[rows], scratch[1].at[step]
            )
            copy.start()
            copies.append(copy)
    for copy in copies:
        copy.wait()


def product(received, by_row):
    out = pl.pallas_call(
        functools.partial(product_kernel, by_row=by_row),
        name="product_out" if by_row else "product_in",
        in_specs=[VMEM],
        out_specs=ANY if by_row else VMEM,
        out_shape=(pltpu.HBM if by_row else pltpu.VMEM)((8, 2, 8, 64, 128), BF16),
        scratch_shapes=[
            pltpu.VMEM((8, 2, 8, 64, 128), BF16),
            pltpu.SemaphoreType.DMA((4,)),
        ]
        if by_row
        else [],
        compiler_params=params(PRODUCT_MIB),
        cost_estimate=cost(2 << 30, 6 << 20),
    )(received)
    return out.reshape(128, 64, 128)


def scale_hidden(hidden_ref, first, spread):
    total = jnp.zeros((ROWS, 128), F32)
    squares = jnp.zeros((ROWS, 128), F32)
    for c in range(128):
        values = hidden_ref[c, first : first + ROWS].astype(F32)
        total += values
        squares += values * values
    mean = total * (1.0 / 128)
    factor = lax.rsqrt(squares * (1.0 / 128) - mean * mean + epsilon)
    for c in range(128):
        spread[c * PITCH : c * PITCH + ROWS, :] = (
            hidden_ref[c, first : first + ROWS].astype(F32) - mean
        ) * factor
    return jnp.concatenate(
        [spread[pl.ds(r, 128, stride=PITCH), :] for r in range(ROWS)], 1
    ).astype(BF16)


def both_halves(rep_ref, mine, other):
    first = rep_ref[0] == 0
    return jnp.concatenate(
        [jnp.where(first, mine, other), jnp.where(first, other, mine)], 0
    )


def by_source(weights):
    rows = weights.astype(F32)
    return jnp.concatenate(
        [rows[p * 64 + r * 8 : p * 64 + r * 8 + 8] for r in range(8) for p in range(2)], 0
    ).astype(BF16)


def middle_kernel(
    rep_ref, hidden_ref, state_ref, gate_ref, mine_ref, other_ref, w_gate_ref, new_ref,
    new_gate_ref, out_ref, spread, sides, old_state, old_gate, load_sems,
):
    loads = []
    for first in range(0, 64, ROWS):
        part = pl.ds(first * 128, ROWS * 128)
        loads.append(
            [
                pltpu.make_async_copy(
                    source.at[:, part], target.at[:, part], load_sems.at[n, first // ROWS]
                )
                for n, (source, target) in enumerate(
                    ((state_ref, old_state), (gate_ref, old_gate))
                )
            ]
        )
    for load in loads[0] + loads[1]:
        load.start()
    w_out = by_source(both_halves(rep_ref, mine_ref[256:320], other_ref[256:320]))
    weights = both_halves(rep_ref, mine_ref[:256], other_ref[:256])
    for first in range(0, 64, ROWS):
        where = slice(first * 128, (first + ROWS) * 128)
        scaled = scale_hidden(hidden_ref, first, spread)
        projected = lax.dot_general(w_out, scaled, TN, preferred_element_type=F32)
        step = first // ROWS
        for load in loads[step]:
            load.wait()
        if step + 2 < len(loads):
            for load in loads[step + 2]:
                load.start()
        state = old_state[:, where].astype(F32) + old_gate[:, where].astype(F32) * projected
        new_ref[:, where] = state.astype(new_ref.dtype)
        normed = normalize(state).astype(BF16)
        half_gate = dot(w_gate_ref[...], normed)
        new_gate_ref[:, where] = (0.5 + 0.5 * jnp.tanh(half_gate)).astype(BF16)
        linear = dot(weights, normed)
        for half in range(2):
            at = half * 256
            left = gated(linear[at : at + 64], linear[at + 64 : at + 128])
            right = gated(linear[at + 128 : at + 192], linear[at + 192 : at + 256])
            for side, tile in enumerate((left, right)):
                for row in range(ROWS):
                    sides[side, pl.ds(half * 64 * PITCH + row, 64, stride=PITCH), :] = tile[
                        :, row * 128 : (row + 1) * 128
                    ]
        for side in range(2):
            for c in range(128):
                out_ref[c, side, first : first + ROWS] = sides[
                    side, c * PITCH : c * PITCH + ROWS, :
                ].astype(BF16)


def middle(rep, hidden, state, gate, mine, other, w_gate):
    return pl.pallas_call(
        middle_kernel,
        name="middle",
        in_specs=[SMEM, VMEM, ANY, ANY, VMEM, VMEM, VMEM],
        out_specs=[VMEM, VMEM, VMEM],
        out_shape=[
            jax.ShapeDtypeStruct((128, 8192), BF16),
            jax.ShapeDtypeStruct((128, 8192), BF16),
            pltpu.VMEM((128, 2, 64, 128), BF16),
        ],
        scratch_shapes=[
            pltpu.VMEM((129 * PITCH, 128), F32),
            pltpu.VMEM((2, 129 * PITCH, 128), F32),
            pltpu.VMEM((128, 8192), BF16),
            pltpu.VMEM((128, 8192), BF16),
            pltpu.SemaphoreType.DMA((2, 64 // ROWS)),
        ],
        compiler_params=params(MIDDLE_MIB),
        cost_estimate=cost(8192 * 128 * 640 * 2, 14 << 20, 1 << 21),
    )(rep, hidden, state, gate, mine, other, w_gate)


def finish_kernel(
    rep_ref, hidden_ref, state_ref, gate_ref, mine_ref, other_ref, w_in_ref, w_down_ref,
    out_ref, spread, state_scr, normed_scr, turned, packed, sems,
):
    w_out = both_halves(rep_ref, mine_ref[320:], other_ref[320:])
    w_half_gate = (w_in_ref[:512] * 0.5).astype(BF16)
    group = 8
    copies = []
    for first in range(0, 64, ROWS):
        where = slice(first * 128, (first + ROWS) * 128)
        scaled = scale_hidden(hidden_ref, first, spread)
        projected = lax.dot_general(w_out, scaled, TN, preferred_element_type=F32)
        state = state_ref[:, where].astype(F32) + gate_ref[:, where].astype(F32) * projected
        state_scr[...] = state
        normed_scr[...] = normalize(state).astype(BF16)
        for start in range(0, ROWS, group):
            part = slice(start * 128, (start + group) * 128)
            normed = normed_scr[:, part]
            half_gate = dot(w_half_gate, normed).astype(BF16)
            linear = dot(w_in_ref[512:], normed).astype(BF16)
            active = gated(half_gate, half_gate) * linear
            updated = state_scr[:, part] + dot(w_down_ref[...], active)
            for row in range(group):
                turned[pl.ds(start + row, 128, stride=PITCH), :] = updated[
                    :, row * 128 : (row + 1) * 128
                ].T
        for i in range(128):
            packed[i, first : first + ROWS] = turned[i * PITCH : i * PITCH + ROWS, :].astype(
                BF16
            )
        rows = pl.ds(first, ROWS)
        copy = pltpu.make_async_copy(
            packed.at[:, rows], out_ref.at[:, rows], sems.at[first // ROWS]
        )
        copy.start()
        copies.append(copy)
    for copy in copies:
        copy.wait()


def finish(rep, hidden, state, gate, mine, other, w_in, w_down):
    return pl.pallas_call(
        finish_kernel,
        name="finish",
        in_specs=[SMEM] + [VMEM] * 7,
        out_specs=ANY,
        out_shape=pltpu.HBM((128, 64, 128), BF16),
        scratch_shapes=[
            pltpu.VMEM((129 * PITCH, 128), F32),
            pltpu.VMEM((128, ROWS * 128), F32),
            pltpu.VMEM((128, ROWS * 128), BF16),
            pltpu.VMEM((129 * PITCH, 128), F32),
            pltpu.VMEM((128, 64, 128), BF16),
            pltpu.SemaphoreType.DMA((64 // ROWS,)),
        ],
        compiler_params=params(FINISH_MIB),
        cost_estimate=cost(8192 * 128 * 1664 * 2, 10 << 20, 1 << 22),
    )(rep, hidden, state, gate, mine, other, w_in, w_down)


def exchange(values, axes):
    return lax.all_to_all(values, axes, split_axis=0, concat_axis=0, tiled=True)


def near(values):
    return pltpu.with_memory_space_constraint(values, pltpu.VMEM)


def far(values):
    return pltpu.with_memory_space_constraint(values, pltpu.HBM)


def on_device(
    pair, w_left, w_left_gate, w_right, w_right_gate, w_gate, w_out, w_trans_in, w_trans_out
):
    rep = lax.axis_index("rep").astype(jnp.int32).reshape(1)
    everywhere = ("row", "rep", "col")
    projections = [
        w.transpose(0, 2, 1) for w in (w_left, w_left_gate, w_right, w_right_gate)
    ]
    sides = front(pair, projections)
    sides, rep = lax.optimization_barrier((sides, rep))
    received = exchange(sides, ("row", "col"))

    products = product(near(received.reshape(8, 8, 2, 128, 128)), True)
    products, pair, w_gate, w_out, w_trans_in, w_trans_out, *projections = (
        lax.optimization_barrier(
            (products, pair, w_gate, w_out, w_trans_in, w_trans_out, *projections)
        )
    )
    hidden = exchange(products, everywhere)

    mine = jnp.concatenate(
        [(w[1] * 0.5).astype(BF16) for w in projections] + [w_out[0], w_out[1]], 0
    )
    other = lax.ppermute(mine, "rep", [(0, 1), (1, 0)])
    gates = (w_gate * 0.5).astype(BF16).transpose(0, 2, 1)
    w_in = w_trans_in.T
    w_down = w_trans_out.T
    state, gate = turn(rep, pair, gates[0])
    hidden, state, gate, gates, w_in, w_down, mine, other = lax.optimization_barrier(
        (hidden, state, gate, gates, w_in, w_down, mine, other)
    )

    state, gate, sides = middle(rep, near(hidden), far(state), far(gate), mine, other, gates[1])
    received = exchange(sides, everywhere)
    hidden = exchange(product(near(received.reshape(8, 2, 8, 2, 64, 128)), False), everywhere)
    return finish(rep, near(hidden), state, gate, mine, other, w_in, w_down)


def solution(mesh):
    placed = (
        P("row", "col", None),
        P(None, None, "rep"),
        P(None, None, "rep"),
        P(None, None, "rep"),
        P(None, None, "rep"),
        P(),
        P(None, "rep", None),
        P(),
        P(),
    )
    return jax.shard_map(
        on_device,
        mesh=mesh,
        in_specs=placed,
        out_specs=P("row", ("col", "rep"), None),
        check_vma=False,
    )
```
